512 devices in a mesh: row: 32 (over z_hi, y, core), col: 16 (over x, z_lo).
Axes of the slice: x: 4, y: 8, z: 8 (z_hi: 2, z_lo: 4; z = z_hi * 4 + z_lo), core: 2. Of those that a mesh axis runs over, the one named last changes fastest.
Arguments:
- coherency: bfloat16 [8, 16, 1, 16, 512, 512], P(None, None, None, 'col', 'row'), may hold values from -6 to 6
- visibilities: float32 [8, 1, 16, 512, 512], P(None, None, 'col', 'row'), may hold values from -24 to 24
- flags: int32 [1, 16, 512, 512], P(None, 'col', 'row'), may hold values 0 or 1
- gains: float32 [8, 16, 16, 512], P(None, None, 'col', 'row'), may hold values from -4 to 4
Outputs:
- residual: float32 [8, 1, 16, 512, 512], P(None, None, 'col', 'row')
- new_gains: float32 [8, 16, 16, 512], P(None, None, 'col', 'row')
The draws below stay inside these ranges and needn't reach their ends.
Inputs may be any that keep to these rules, and one draw needn't show every extreme that they name: `flags`: 1 keeps a sample, 0 drops it.
All inputs are finite; a program needn't handle non-finite values. No bound on the sum of `flags` on one device may be relied on, other than what follows from the above.
Results may differ from the reference program's by a relative error of at most 0.0003.
Values sent between devices are 32-bit elements; how exact they have to be, the bound alone decides.
A program may use at most 128 MiB of HBM per device.

```python
import jax
import jax.numpy as jnp
from jax import lax

S = 512
DIR = 16
CH = 16
TS = 1
SQ = 32
CB = 16
N_ROW = 32


def place_ends(entries, key, low, top_value):
    dims = entries.shape
    place = [jax.random.randint(jax.random.fold_in(key, axis), (), 0, dims[axis]) for axis in range(len(dims))]
    entries = entries.at[tuple(place)].set(low)
    longest = dims.index(max(dims))
    place[longest] = (place[longest] + 1) % dims[longest]
    return entries.at[tuple(place)].set(top_value)


def level_of(own_key, shape, cuts, smallest, top_value):
    gain = 1.0
    for axis_at, blocks in cuts:
        heights = jax.random.uniform(jax.random.fold_in(jax.random.fold_in(own_key, 6), axis_at), (blocks,), jnp.float32, smallest / len(cuts), top_value / len(cuts))
        gain = gain * jnp.repeat(jnp.exp(heights), shape[axis_at] // blocks).reshape((-1,) + (1,) * (len(shape) - 1 - axis_at))
    return gain


def normal_values(rng, shape, scale, most, shards=(), held_as=jnp.bfloat16):
    factor_of = level_of(rng, shape, shards, -0.22, 0.18) if shards else 1.0
    values = jax.random.normal(rng, shape, jnp.float32) * scale * factor_of
    return jnp.minimum(jnp.maximum(values, -most), most).astype(held_as)


def setup_inputs(seed: int = 0) -> dict:
    keys = jax.random.split(jax.random.key(seed), 5)
    return {
        "coherency": normal_values(keys[0], (8, DIR, TS, CB, S, CH * SQ), 1.0, 6.0, ((3, 16), (4, 32))),
        "visibilities": normal_values(keys[1], (8, TS, CB, S, CH * SQ), 4.0, 24.0, ((2, 16), (3, 32)), jnp.float32),
        "flags": place_ends((jax.random.randint(keys[2], (TS, CB, S, CH * SQ), 0, 10) < 9).astype(jnp.int32), jax.random.fold_in(keys[2], 1), 0, 1),
        "gains": normal_values(keys[3], (8, DIR, CH, S), 0.7, 4.0, ((2, 16), (3, 32)), jnp.float32),
    }


epsilon = 1e-6


def split_planes(packed, widen):
    return [[(widen(packed[4 * line + 2 * column]), widen(packed[4 * line + 2 * column + 1])) for column in range(2)] for line in range(2)]


def stack_planes(matrix):
    return jnp.stack([matrix[line][column][part] for line in range(2) for column in range(2) for part in range(2)], axis=0)


def complex_mul(first, second):
    return (first[0] * second[0] - first[1] * second[1], first[0] * second[1] + first[1] * second[0])


def complex_mul_conj(first, second):
    return (first[0] * second[0] + first[1] * second[1], first[1] * second[0] - first[0] * second[1])


def complex_add(first, second):
    return (first[0] + second[0], first[1] + second[1])


def matrix_product(first, second):
    return [[complex_add(complex_mul(first[line][0], second[0][column]), complex_mul(first[line][1], second[1][column])) for column in range(2)] for line in range(2)]


def product_herm(first, second):
    return [[complex_add(complex_mul_conj(first[line][0], second[column][0]), complex_mul_conj(first[line][1], second[column][1])) for column in range(2)] for line in range(2)]


def herm_product(first, second):
    return [[complex_add(complex_mul_conj(second[0][column], first[0][line]), complex_mul_conj(second[1][column], first[1][line])) for column in range(2)] for line in range(2)]


def sum_squares(matrix):
    total = matrix[0][0][0] * matrix[0][0][0]
    for line in range(2):
        for column in range(2):
            for part in range(2):
                if line + column + part > 0:
                    total = total + matrix[line][column][part] * matrix[line][column][part]
    return total


def block_terms(row_jones, sky_block, col_jones, observed, weight):
    quota = col_jones.shape[3]
    channels = col_jones.shape[2]
    rows = row_jones.shape[3]

    def widen_row(plane):
        return jnp.repeat(jnp.swapaxes(plane, 1, 2), quota, axis=2)[:, None, :, :]

    def widen_col(plane):
        return plane.reshape(plane.shape[0], channels * quota)[:, None, None, :]

    left = split_planes(row_jones, widen_row)
    right = split_planes(col_jones, widen_col)
    sky = split_planes(sky_block, lambda plane: plane.astype(jnp.float32))
    front = matrix_product(left, sky)
    behind = product_herm(sky, right)
    model_sum = stack_planes(product_herm(front, right)).sum(axis=1)
    residual = weight[None] * (observed - model_sum)
    error = split_planes(residual, lambda plane: plane[None])
    row_full = stack_planes(product_herm(error, behind))
    row_grad = -jnp.swapaxes(row_full.reshape(row_full.shape[:4] + (channels, quota)).sum(axis=(2, 5)), 2, 3)
    col_full = stack_planes(herm_product(error, front)).sum(axis=(2, 3))
    col_grad = -col_full.reshape(8, col_full.shape[1], channels, quota)
    behind_weight = weight[None] * sum_squares(behind)
    row_curv = jnp.swapaxes(behind_weight.reshape(behind_weight.shape[:3] + (channels, quota)).sum(axis=(1, 4)), 1, 2)[None]
    front_weight = (weight[None] * sum_squares(front)).sum(axis=(1, 2))
    col_curv = front_weight.reshape(front_weight.shape[0], channels, quota)[None]
    return residual, row_grad, row_curv, col_grad, col_curv


def reference(coherency, visibilities, flags, gains):
    block = S // N_ROW
    count = S // block
    sky_all = coherency.reshape(8, DIR, TS, CB, S, CH, SQ).transpose(0, 1, 2, 4, 5, 3, 6).reshape(8, DIR, TS, S, CH * S)
    seen_all = visibilities.reshape(8, TS, CB, S, CH, SQ).transpose(0, 1, 3, 4, 2, 5).reshape(8, TS, S, CH * S)
    flag_all = flags.reshape(TS, CB, S, CH, SQ).transpose(0, 2, 3, 1, 4).reshape(TS, S, CH * S)
    station = jnp.arange(CH * S, dtype=jnp.int32) % S

    def step(carry, index):
        col_total, curv_total = carry
        start = (index * block).astype(jnp.int32)
        sky_block = lax.dynamic_slice_in_dim(sky_all, start, block, 3)
        observed = lax.dynamic_slice_in_dim(seen_all, start, block, 2)
        flag_block = lax.dynamic_slice_in_dim(flag_all, start, block, 1)
        row_jones = lax.dynamic_slice_in_dim(gains, start, block, 3)
        rows = start + jnp.arange(block, dtype=jnp.int32)
        weight = flag_block.astype(jnp.float32) * (rows[:, None] != station[None, :]).astype(jnp.float32)[None]
        residual, row_grad, row_curv, grad_part, curv_part = block_terms(row_jones, sky_block, gains, observed, weight)
        return (col_total + grad_part, curv_total + curv_part), (residual, row_grad, row_curv)

    start_carry = (jnp.zeros((8, DIR, CH, S), jnp.float32), jnp.zeros((1, DIR, CH, S), jnp.float32))
    (col_grad, col_curv), (residual, row_grad, row_curv) = lax.scan(step, start_carry, jnp.arange(count, dtype=jnp.int32))
    residual = jnp.moveaxis(residual, 0, 2).reshape(8, TS, S, CH, CB, SQ)
    residual = residual.transpose(0, 1, 4, 2, 3, 5).reshape(8, TS, CB, S, CH * SQ)
    row_grad = jnp.moveaxis(row_grad, 0, 3).reshape(8, DIR, CH, S)
    row_curv = jnp.moveaxis(row_curv, 0, 3).reshape(1, DIR, CH, S)
    total_grad = row_grad + col_grad
    total_curv = row_curv + col_curv
    new_gains = gains - total_grad / (total_curv + epsilon)
    return (residual, new_gains)
```

```python
import functools

import jax
import jax.numpy as jnp
from jax import lax
from jax.experimental import pallas as pl
from jax.experimental.pallas import tpu as pltpu
from jax.sharding import PartitionSpec as P

epsilon = 1e-06
MESH = pl.DeviceIdType.MESH
LANES = 128
QUOTA = 32
FAN = LANES // QUOTA
SLOT = 24
USED = 18
BLOCK = 16


def mul(first, second):
    out = []
    for a in range(2):
        for b in range(2):
            re = im = None
            for k in range(2):
                fr, fi = first[4 * a + 2 * k], first[4 * a + 2 * k + 1]
                sr, si = second[4 * k + 2 * b], second[4 * k + 2 * b + 1]
                r, i = fr * sr - fi * si, fr * si + fi * sr
                re, im = (r, i) if re is None else (re + r, im + i)
            out += [re, im]
    return out


def mul_herm(first, second, total=None):
    out = []
    for a in range(2):
        for c in range(2):
            re = im = None
            if total is not None:
                re, im = total[4 * a + 2 * c], total[4 * a + 2 * c + 1]
            for b in range(2):
                fr, fi = first[4 * a + 2 * b], first[4 * a + 2 * b + 1]
                sr, si = second[4 * c + 2 * b], second[4 * c + 2 * b + 1]
                r, i = fr * sr + fi * si, fi * sr - fr * si
                re, im = (r, i) if re is None else (re + r, im + i)
            out += [re, im]
    return out


def herm_mul(first, second):
    out = []
    for a in range(2):
        for c in range(2):
            re = im = None
            for b in range(2):
                fr, fi = first[4 * b + 2 * a], first[4 * b + 2 * a + 1]
                sr, si = second[4 * b + 2 * c], second[4 * b + 2 * c + 1]
                r, i = sr * fr + si * fi, si * fr - sr * fi
                re, im = (r, i) if re is None else (re + r, im + i)
            out += [re, im]
    return out


def squares(planes):
    total = planes[0] * planes[0]
    for plane in planes[1:]:
        total = total + plane * plane
    return total


def swap_bits(x, row_bit, lane_bit, row_of, block_of):
    row_high = (row_of >> row_bit) & 1
    lane_high = (block_of >> lane_bit) & 1
    rows, lanes = 1 << row_bit, 16 << lane_bit
    up = pltpu.roll(pltpu.roll(x, 8 - rows, 0), lanes, 1)
    down = pltpu.roll(pltpu.roll(x, rows, 0), LANES - lanes, 1)
    return jnp.where(row_high == lane_high, x, jnp.where(row_high == 0, up, down))


def place_of(low):
    return (low % 2) * 4 + ((low // 4) % 2) * 2 + (low // 2) % 2


SWAPS = ((2, 0), (1, 2), (0, 1))


def kernel(
    n_col, n_dir, n_p,
    sky_ref, seen_ref, flag_ref, gain_ref, res_out, gain_out,
    sky_v, seen_v, flag_v, gain_v, wide_v, send_v, row_v, col_v, part_v, left_v, right_v,
    front_v, wide_sky_v, res_v, prod_v, colsum_v, rmsg_v, cmsg_v, sib_v, rin_v, cin_v, new_v,
    in_sem, r_send, c_send, r_recv, c_recv, relay_send, relay_recv, sib_send, sib_recv,
    ro_send, ro_recv, co_send, co_recv, out_sem,
):
    i, k = lax.axis_index("row"), lax.axis_index("col")
    m, h = i // 2, i % 2
    groups = n_col // FAN
    first_group = k // FAN
    sibling = 2 * m + (1 - h)
    alone = k == m
    f32, bf16 = jnp.float32, jnp.bfloat16

    def lanes_of(g):
        return pl.ds(pl.multiple_of(g * LANES, LANES), LANES)

    def rows_at(ref, start, size):
        return ref.at[pl.ds(pl.multiple_of(start, 8), size)]

    gain_copy = pltpu.make_async_copy(gain_ref, gain_v, in_sem.at[0])
    gain_copy.start()
    seen_copy = pltpu.make_async_copy(seen_ref, seen_v, in_sem.at[1])
    flag_copy = pltpu.make_async_copy(flag_ref, flag_v, in_sem.at[2])

    def sky_copy(g):
        return pltpu.make_async_copy(
            sky_ref.at[:, :, :, lanes_of(g)], sky_v.at[g], in_sem.at[3 + g]
        )

    barrier = pltpu.get_barrier_semaphore()

    def signal(row, col):
        pl.semaphore_signal(barrier, inc=1, device_id=(row, col), device_id_type=MESH)

    signal(sibling, k)

    @pl.loop(1, n_col)
    def _(o):
        signal(i, (k + o) % n_col)

    @pl.loop(0, n_col)
    def _(o):
        c = (m + o) % n_col

        @pl.when(jnp.logical_not(jnp.logical_and(alone, c == m)))
        def _():
            signal(2 * k + h, c)

    for t in range(groups):
        sky_copy((first_group + t) % groups).start()
    seen_copy.start()
    flag_copy.start()

    gain_copy.wait()
    wide_v[...] = jnp.zeros_like(wide_v)
    wide_v[:, 0:16] = gain_v[...]
    own = wide_v[pl.ds(0, BLOCK, stride=8), :]
    for j in range(1, 8):
        own = own + pltpu.roll(wide_v[pl.ds(j, BLOCK, stride=8), :], 16 * j, 1)
    send_v[...] = own

    pl.semaphore_wait(barrier, 2 * n_col - alone.astype(jnp.int32))

    def col_row(c, half):
        return (((c // FAN) * 2 + half) * FAN + c % FAN) * BLOCK

    def send_row(c):
        pltpu.make_async_remote_copy(
            src_ref=send_v, dst_ref=rows_at(row_v, k * BLOCK, BLOCK),
            send_sem=r_send.at[0], recv_sem=r_recv.at[k // FAN],
            device_id=(i, c), device_id_type=MESH,
        ).start()

    def send_col(target):
        pltpu.make_async_remote_copy(
            src_ref=send_v, dst_ref=rows_at(col_v, col_row(k, h), BLOCK),
            send_sem=c_send.at[0], recv_sem=c_recv.at[k // FAN],
            device_id=(2 * target + h, m), device_id_type=MESH,
        ).start()

    pltpu.make_async_copy(
        send_v, rows_at(row_v, k * BLOCK, BLOCK), r_recv.at[k // FAN]
    ).start()

    @pl.when(alone)
    def _():
        pltpu.make_async_copy(
            send_v, rows_at(col_v, col_row(k, h), BLOCK), c_recv.at[k // FAN]
        ).start()

    @pl.loop(1, FAN)
    def _(o):
        send_row(first_group * FAN + (k + o) % FAN)

    @pl.loop(1, n_col)
    def _(o):
        send_col((m + o) % n_col)

    @pl.when(jnp.logical_not(alone))
    def _():
        send_col(m)

    @pl.loop(FAN, n_col)
    def _(o):
        send_row(((first_group + groups - o // FAN) % groups) * FAN + (k + o) % FAN)

    def relay(g, half):
        block = rows_at(col_v, (g * 2 + half) * FAN * BLOCK, FAN * BLOCK)
        return pltpu.make_async_remote_copy(
            src_ref=block, dst_ref=block,
            send_sem=relay_send.at[g], recv_sem=relay_recv.at[g],
            device_id=(sibling, k), device_id_type=MESH,
        )

    def pass_on(g):
        block = rows_at(col_v, (g * 2 + h) * FAN * BLOCK, FAN * BLOCK)
        pltpu.make_async_copy(block, block, c_recv.at[g]).wait()
        relay(g, h).start()

    def exchange(g):
        return pltpu.make_async_remote_copy(
            src_ref=rows_at(cmsg_v, (g * 2 + 1 - h) * FAN * SLOT, FAN * SLOT),
            dst_ref=rows_at(sib_v, g * FAN * SLOT, FAN * SLOT),
            send_sem=sib_send.at[g], recv_sem=sib_recv.at[g],
            device_id=(sibling, k), device_id_type=MESH,
        )

    def row_out(c):
        return pltpu.make_async_remote_copy(
            src_ref=rows_at(rmsg_v, c * SLOT, USED), dst_ref=rows_at(rin_v, k * SLOT, USED),
            send_sem=ro_send.at[c], recv_sem=ro_recv.at[k],
            device_id=(i, c), device_id_type=MESH,
        )

    def cmsg_row(c):
        return (((c // FAN) * 2 + h) * FAN + c % FAN) * SLOT

    def col_out(c):
        return pltpu.make_async_remote_copy(
            src_ref=rows_at(cmsg_v, cmsg_row(c), USED), dst_ref=rows_at(cin_v, m * SLOT, USED),
            send_sem=co_send.at[c], recv_sem=co_recv.at[m],
            device_id=(2 * k + h, c), device_id_type=MESH,
        )

    def send_cols(g):
        exchange(g).wait_recv()
        base = pl.multiple_of((g * 2 + h) * FAN * SLOT, 8)
        span = pl.ds(base, FAN * SLOT)
        cmsg_v[span] = cmsg_v[span] + sib_v[pl.ds(pl.multiple_of(g * FAN * SLOT, 8), FAN * SLOT)]

        @pl.loop(0, FAN)
        def _(o):
            c = g * FAN + o

            @pl.when(jnp.logical_and(alone, c == m))
            def _():
                pltpu.make_async_copy(
                    rows_at(cmsg_v, cmsg_row(c), USED), rows_at(cin_v, m * SLOT, USED),
                    co_recv.at[m],
                ).start()

            @pl.when(jnp.logical_not(jnp.logical_and(alone, c == m)))
            def _():
                col_out(c).start()

    row_of = lax.broadcasted_iota(jnp.int32, (8, LANES), 0)
    lane_of = lax.broadcasted_iota(jnp.int32, (8, LANES), 1)
    block_of = lane_of // 16
    low_row = lax.broadcasted_iota(jnp.int32, (16, LANES), 0)
    low_lane = lax.broadcasted_iota(jnp.int32, (16, LANES), 1)
    widen = jnp.where(
        jnp.logical_and(low_lane // QUOTA == low_row % FAN, low_row < 3 * FAN), 1.0, 0.0
    ).astype(bf16)
    sum_row = lax.broadcasted_iota(jnp.int32, (8, 2 * LANES), 0)
    sum_lane = lax.broadcasted_iota(jnp.int32, (8, 2 * LANES), 1)
    gather = jnp.where((sum_lane % LANES) // QUOTA == sum_row, 1.0, 0.0).astype(bf16)

    part_v[3 * FAN * BLOCK :] = jnp.zeros((FAN * BLOCK, LANES), f32)

    pass_on(first_group)

    @pl.loop(0, groups)
    def _(t):
        g = (first_group + t) % groups

        @pl.when(t + 1 < groups)
        def _():
            pass_on((first_group + t + 1) % groups)

        relay(g, 1 - h).wait_recv()
        block = rows_at(row_v, g * FAN * BLOCK, FAN * BLOCK)
        pltpu.make_async_copy(block, block, r_recv.at[g]).wait()

        for r in range(BLOCK):
            x = col_v[pl.ds(g * (2 * FAN * BLOCK) + r, 8, stride=BLOCK), :]
            for row_bit, lane_bit in SWAPS:
                x = swap_bits(x, row_bit, lane_bit, row_of, block_of)
            right_v[8 * r : 8 * r + 8, :] = x

        value = row_v[pl.ds(pl.multiple_of(g * FAN * BLOCK, 8), FAN * BLOCK), :]
        high = value.astype(bf16).astype(f32)
        rest = value - high
        middle = rest.astype(bf16).astype(f32)
        part_v[0 : FAN * BLOCK] = high
        part_v[FAN * BLOCK : 2 * FAN * BLOCK] = middle
        part_v[2 * FAN * BLOCK : 3 * FAN * BLOCK] = rest - middle
        for r in range(BLOCK):
            x = part_v[pl.ds(r, 16, stride=BLOCK), :]
            left_v[r * LANES : (r + 1) * LANES, :] = lax.dot_general(
                x.T.astype(bf16), widen, (((1,), (0,)), ((), ())), preferred_element_type=f32
            )

        @pl.when(t == 0)
        def _():
            seen_copy.wait()
            flag_copy.wait()

        sky_copy(g).wait()

        def right_of(d):
            at = (d // 8) * 8 + place_of(d % 8)
            return [
                jnp.broadcast_to(right_v[pl.ds(plane * n_dir + at, 1), :], (8, LANES))
                for plane in range(8)
            ]

        def model_step(d, total):
            right = right_of(d)
            sky = [sky_v[g, plane, d].astype(f32) for plane in range(8)]
            new = []
            for half in range(2):
                part = [plane[8 * half : 8 * half + 8] for plane in sky]
                left = [
                    left_v[pl.ds(pl.multiple_of((plane * n_dir + d) * n_p + 8 * half, 8), 8), :]
                    for plane in range(8)
                ]
                front = mul(left, part)
                for plane in range(8):
                    front_v[plane, d, 8 * half : 8 * half + 8] = front[plane]
                    wide_sky_v[plane, d, 8 * half : 8 * half + 8] = part[plane]
                new += mul_herm(front, right, total[8 * half : 8 * half + 8])
            return tuple(new)

        zero = jnp.zeros((8, LANES), f32)
        model = lax.fori_loop(0, n_dir, model_step, (zero,) * 16)

        @pl.when(t > 0)
        def _():
            send_cols((first_group + t + groups - 1) % groups)

        lanes = lanes_of(g)
        weight, error = [], []
        for half in range(2):
            rows = i * n_p + 8 * half + row_of
            columns = k * QUOTA + lane_of % QUOTA
            kept = flag_v[8 * half : 8 * half + 8, lanes].astype(f32)
            kept = kept * (rows != columns).astype(f32)
            weight.append(kept)
            for plane in range(8):
                seen = seen_v[plane, 8 * half : 8 * half + 8, lanes]
                value = kept * (seen - model[8 * half + plane])
                error.append(value)
                res_v[plane, 8 * half : 8 * half + 8, lanes] = value
        pltpu.make_async_copy(
            res_v.at[:, :, lanes], res_out.at[:, :, lanes], out_sem.at[g]
        ).start()

        def sum_step(d, carry):
            right = right_of(d)
            rows, cols = [], None
            for half in range(2):
                wrong = error[8 * half : 8 * half + 8]
                sky = [wide_sky_v[plane, d, 8 * half : 8 * half + 8] for plane in range(8)]
                front = [front_v[plane, d, 8 * half : 8 * half + 8] for plane in range(8)]
                behind = mul_herm(sky, right)
                rows.append(mul_herm(wrong, behind) + [weight[half] * squares(behind)])
                col = herm_mul(wrong, front) + [weight[half] * squares(front)]
                cols = col if cols is None else [a + b for a, b in zip(cols, col)]
            at = pl.ds(pl.multiple_of(d * n_p, 16), n_p)
            for plane in range(9):
                x = jnp.concatenate([rows[0][plane], rows[1][plane]], axis=0)
                high = x.astype(bf16)
                prod_v[plane, at, 0:LANES] = high
                prod_v[plane, at, LANES : 2 * LANES] = (x - high.astype(f32)).astype(bf16)
                colsum_v[plane, d] = cols[plane]
            return carry

        lax.fori_loop(0, n_dir, sum_step, 0)

        for plane in range(9):
            x = lax.dot_general(
                gather, prod_v[plane], (((1,), (1,)), ((), ())), preferred_element_type=f32
            )
            for high in range(n_dir // 8):
                rmsg_v[pl.ds(g * FAN * SLOT + 2 * plane + high, FAN, stride=SLOT), :] = x[
                    0:FAN, high * LANES : (high + 1) * LANES
                ]

        @pl.loop(0, FAN)
        def _(o):
            c = g * FAN + o

            @pl.when(c == k)
            def _():
                pltpu.make_async_copy(
                    rows_at(rmsg_v, k * SLOT, USED), rows_at(rin_v, k * SLOT, USED), ro_recv.at[k]
                ).start()

            @pl.when(c != k)
            def _():
                row_out(c).start()

        for plane in range(9):
            for high in range(n_dir // 8):
                items = [None] * 8
                for low in range(8):
                    items[place_of(low)] = colsum_v[plane, 8 * high + low]
                for bit in range(3):
                    up = ((row_of >> bit) & 1) == 1
                    items = [
                        jnp.where(up, b, a) + pltpu.roll(jnp.where(up, a, b), 1 << bit, 0)
                        for a, b in zip(items[0::2], items[1::2])
                    ]
                x = items[0]
                for row_bit, lane_bit in SWAPS:
                    x = swap_bits(x, row_bit, lane_bit, row_of, block_of)
                cmsg_v[pl.ds(g * 2 * FAN * SLOT + 2 * plane + high, 8, stride=SLOT), :] = x
        exchange(g).start()

    send_cols((first_group + groups - 1) % groups)

    def add_up(buffer, sems, source, total):
        at = rows_at(buffer, source * SLOT, USED)
        pltpu.make_async_copy(at, at, sems.at[source]).wait()
        start = pl.multiple_of(source * SLOT, 8)
        return tuple(
            part + buffer[pl.ds(start + 8 * n, size), :]
            for n, (part, size) in enumerate(zip(total, (8, 8, 2)))
        )

    def add_step(o, total):
        total = add_up(rin_v, ro_recv, (k + o) % n_col, total)
        return add_up(cin_v, co_recv, (m + o) % n_col, total)

    zero = jnp.zeros((8, LANES), f32)
    top, bottom, curvature = lax.fori_loop(
        0, n_col, add_step, (zero, zero, jnp.zeros((2, LANES), f32))
    )
    divisor = jnp.where(
        row_of % 2 == 0,
        jnp.broadcast_to(curvature[0:1], (8, LANES)),
        jnp.broadcast_to(curvature[1:2], (8, LANES)),
    ) + epsilon
    fresh = send_v[...] + jnp.concatenate([top / divisor, bottom / divisor], axis=0)
    for j in range(8):
        wide_v[pl.ds(j, BLOCK, stride=8), :] = fresh if j == 0 else pltpu.roll(fresh, LANES - 16 * j, 1)
    new_v[...] = wide_v[:, 0:16]
    new_copy = pltpu.make_async_copy(new_v, gain_out, out_sem.at[groups])
    new_copy.start()

    sent = rows_at(row_v, 0, (n_col - 1) * BLOCK)
    pltpu.make_async_copy(sent, sent, r_send.at[0]).wait()

    @pl.when(alone)
    def _():
        sent = rows_at(row_v, 0, (n_col - 1) * BLOCK)
        pltpu.make_async_copy(sent, sent, c_send.at[0]).wait()

    @pl.when(jnp.logical_not(alone))
    def _():
        sent = rows_at(row_v, 0, n_col * BLOCK)
        pltpu.make_async_copy(sent, sent, c_send.at[0]).wait()

    @pl.loop(0, groups)
    def _(g):
        relay(g, h).wait_send()
        exchange(g).wait_send()
        lanes = lanes_of(g)
        pltpu.make_async_copy(
            res_v.at[:, :, lanes], res_out.at[:, :, lanes], out_sem.at[g]
        ).wait()

    @pl.loop(0, n_col)
    def _(c):
        @pl.when(c != k)
        def _():
            row_out(c).wait_send()

        @pl.when(jnp.logical_not(jnp.logical_and(alone, c == m)))
        def _():
            col_out(c).wait_send()

    new_copy.wait()


def on_device(coherency, visibilities, flags, gains):
    n_col = lax.axis_size("col")
    n_dir, n_p, width = coherency.shape[1], coherency.shape[4], coherency.shape[5]
    groups = width // LANES
    sky = coherency.reshape(8, n_dir, n_p, width)
    seen = visibilities.reshape(8, n_p, width)
    flag = flags.reshape(n_p, width)
    mine = gains.reshape(8 * n_dir, n_p)
    f32, bf16 = jnp.float32, jnp.bfloat16
    any_spec = pl.BlockSpec(memory_space=pl.ANY)
    dma = pltpu.SemaphoreType.DMA
    residual, fresh = pl.pallas_call(
        functools.partial(kernel, n_col, n_dir, n_p),
        out_shape=(
            jax.ShapeDtypeStruct(seen.shape, f32),
            jax.ShapeDtypeStruct(mine.shape, f32),
        ),
        in_specs=[any_spec] * 4,
        out_specs=(any_spec, any_spec),
        scratch_shapes=[
            pltpu.VMEM((groups, 8, n_dir, n_p, LANES), bf16),
            pltpu.VMEM(seen.shape, f32),
            pltpu.VMEM(flag.shape, jnp.int32),
            pltpu.VMEM(mine.shape, f32),
            pltpu.VMEM((8 * n_dir, LANES), f32),
            pltpu.VMEM((BLOCK, LANES), f32),
            pltpu.VMEM((n_col * BLOCK, LANES), f32),
            pltpu.VMEM((2 * n_col * BLOCK, LANES), f32),
            pltpu.VMEM((4 * FAN * BLOCK, LANES), f32),
            pltpu.VMEM((8 * n_dir * n_p, LANES), f32),
            pltpu.VMEM((8 * n_dir, LANES), f32),
            pltpu.VMEM((8, n_dir, n_p, LANES), f32),
            pltpu.VMEM((8, n_dir, n_p, LANES), f32),
            pltpu.VMEM(seen.shape, f32),
            pltpu.VMEM((9, n_dir * n_p, 2 * LANES), bf16),
            pltpu.VMEM((9, n_dir, 8, LANES), f32),
            pltpu.VMEM((n_col * SLOT, LANES), f32),
            pltpu.VMEM((2 * n_col * SLOT, LANES), f32),
            pltpu.VMEM((n_col * SLOT, LANES), f32),
            pltpu.VMEM((n_col * SLOT, LANES), f32),
            pltpu.VMEM((n_col * SLOT, LANES), f32),
            pltpu.VMEM(mine.shape, f32),
            dma((3 + groups,)),
            dma((1,)),
            dma((1,)),
            dma((groups,)),
            dma((groups,)),
            dma((groups,)),
            dma((groups,)),
            dma((groups,)),
            dma((groups,)),
            dma((n_col,)),
            dma((n_col,)),
            dma((n_col,)),
            dma((n_col,)),
            dma((groups + 1,)),
        ],
        compiler_params=pltpu.CompilerParams(
            collective_id=0, has_side_effects=True, vmem_limit_bytes=56 * 1024 * 1024
        ),
    )(sky, seen, flag, mine)
    return residual.reshape(visibilities.shape), fresh.reshape(gains.shape)


def solution(mesh):
    return jax.shard_map(
        on_device,
        mesh=mesh,
        in_specs=(
            P(None, None, None, "col", "row", None),
            P(None, None, "col", "row", None),
            P(None, "col", "row", None),
            P(None, None, "col", "row"),
        ),
        out_specs=(P(None, None, "col", "row", None), P(None, None, "col", "row")),
        check_vma=False,
    )
```

```python
import functools

import jax
import jax.numpy as jnp
from jax import lax
from jax.experimental import pallas as pl
from jax.experimental.pallas import tpu as pltpu
from jax.sharding import PartitionSpec as P

epsilon = 1e-06
MESH = pl.DeviceIdType.MESH
LANES = 128
QUOTA = 32
FAN = LANES // QUOTA
SLOT = 24
MODEL_UNROLL = 4
SUM_UNROLL = 4
USED = 18
BLOCK = 16


def mul(first, second):
    out = []
    for a in range(2):
        for b in range(2):
            re = im = None
            for k in range(2):
                fr, fi = first[4 * a + 2 * k], first[4 * a + 2 * k + 1]
                sr, si = second[4 * k + 2 * b], second[4 * k + 2 * b + 1]
                r, i = fr * sr - fi * si, fr * si + fi * sr
                re, im = (r, i) if re is None else (re + r, im + i)
            out += [re, im]
    return out


def mul_herm(first, second, total=None):
    out = []
    for a in range(2):
        for c in range(2):
            re = im = None
            if total is not None:
                re, im = total[4 * a + 2 * c], total[4 * a + 2 * c + 1]
            for b in range(2):
                fr, fi = first[4 * a + 2 * b], first[4 * a + 2 * b + 1]
                sr, si = second[4 * c + 2 * b], second[4 * c + 2 * b + 1]
                r, i = fr * sr + fi * si, fi * sr - fr * si
                re, im = (r, i) if re is None else (re + r, im + i)
            out += [re, im]
    return out


def herm_mul(first, second):
    out = []
    for a in range(2):
        for c in range(2):
            re = im = None
            for b in range(2):
                fr, fi = first[4 * b + 2 * a], first[4 * b + 2 * a + 1]
                sr, si = second[4 * b + 2 * c], second[4 * b + 2 * c + 1]
                r, i = sr * fr + si * fi, si * fr - sr * fi
                re, im = (r, i) if re is None else (re + r, im + i)
            out += [re, im]
    return out


def squares(planes):
    total = planes[0] * planes[0]
    for plane in planes[1:]:
        total = total + plane * plane
    return total


def swap_bits(x, row_bit, lane_bit, row_of, block_of):
    row_high = (row_of >> row_bit) & 1
    lane_high = (block_of >> lane_bit) & 1
    rows, lanes = 1 << row_bit, 16 << lane_bit
    up = pltpu.roll(pltpu.roll(x, 8 - rows, 0), lanes, 1)
    down = pltpu.roll(pltpu.roll(x, rows, 0), LANES - lanes, 1)
    return jnp.where(row_high == lane_high, x, jnp.where(row_high == 0, up, down))


def place_of(low):
    return (low % 2) * 4 + ((low // 4) % 2) * 2 + (low // 2) % 2


SWAPS = ((2, 0), (1, 2), (0, 1))


def kernel(
    n_col, n_dir, n_p,
    sky_ref, seen_ref, flag_ref, gain_ref, res_out, gain_out,
    sky_v, seen_v, flag_v, gain_v, wide_v, send_v, row_v, col_v, part_v, left_v, right_v,
    front_v, wide_sky_v, res_v, prod_v, colsum_v, rmsg_v, cmsg_v, sib_v, rin_v, mid_v, cin_v, new_v,
    in_sem, r_send, c_send, r_recv, c_recv, relay_send, relay_recv, sib_send, sib_recv,
    ro_send, ro_recv, co_send, mid_recv, on_send, cin_recv, out_sem,
):
    i, k = lax.axis_index("row"), lax.axis_index("col")
    m, h = i // 2, i % 2
    groups = n_col // FAN
    first_group = k // FAN
    sibling = 2 * m + (1 - h)
    alone = k == m
    f32, bf16 = jnp.float32, jnp.bfloat16

    def lanes_of(g):
        return pl.ds(pl.multiple_of(g * LANES, LANES), LANES)

    def rows_at(ref, start, size):
        return ref.at[pl.ds(pl.multiple_of(start, 8), size)]

    gain_copy = pltpu.make_async_copy(gain_ref, gain_v, in_sem.at[0])
    gain_copy.start()
    seen_copy = pltpu.make_async_copy(seen_ref, seen_v, in_sem.at[1])
    flag_copy = pltpu.make_async_copy(flag_ref, flag_v, in_sem.at[2])

    def sky_copy(g):
        return pltpu.make_async_copy(
            sky_ref.at[:, :, :, lanes_of(g)], sky_v.at[g], in_sem.at[3 + g]
        )

    barrier = pltpu.get_barrier_semaphore()

    def signal(row, col):
        pl.semaphore_signal(barrier, inc=1, device_id=(row, col), device_id_type=MESH)

    signal(sibling, k)

    @pl.loop(1, n_col)
    def _(o):
        signal(i, (k + o) % n_col)

    @pl.loop(0, n_col)
    def _(o):
        c = (m + o) % n_col

        @pl.when(jnp.logical_not(jnp.logical_and(alone, c == m)))
        def _():
            signal(2 * k + h, c)

    for t in range(groups):
        sky_copy((first_group + t) % groups).start()
    seen_copy.start()
    flag_copy.start()

    gain_copy.wait()
    wide_v[...] = jnp.zeros_like(wide_v)
    wide_v[:, 0:16] = gain_v[...]
    own = wide_v[pl.ds(0, BLOCK, stride=8), :]
    for j in range(1, 8):
        own = own + pltpu.roll(wide_v[pl.ds(j, BLOCK, stride=8), :], 16 * j, 1)
    send_v[...] = own

    pl.semaphore_wait(barrier, 2 * n_col - alone.astype(jnp.int32))

    def col_row(c, half):
        return (((c // FAN) * 2 + half) * FAN + c % FAN) * BLOCK

    def send_row(c):
        pltpu.make_async_remote_copy(
            src_ref=send_v, dst_ref=rows_at(row_v, k * BLOCK, BLOCK),
            send_sem=r_send.at[0], recv_sem=r_recv.at[k // FAN],
            device_id=(i, c), device_id_type=MESH,
        ).start()

    def send_col(target):
        pltpu.make_async_remote_copy(
            src_ref=send_v, dst_ref=rows_at(col_v, col_row(k, h), BLOCK),
            send_sem=c_send.at[0], recv_sem=c_recv.at[k // FAN],
            device_id=(2 * target + h, m), device_id_type=MESH,
        ).start()

    pltpu.make_async_copy(
        send_v, rows_at(row_v, k * BLOCK, BLOCK), r_recv.at[k // FAN]
    ).start()

    @pl.when(alone)
    def _():
        pltpu.make_async_copy(
            send_v, rows_at(col_v, col_row(k, h), BLOCK), c_recv.at[k // FAN]
        ).start()

    for o in range(1, FAN):
        send_row(first_group * FAN + (k + o) % FAN)

    for o in range(1, n_col):
        send_col((m + o) % n_col)

    @pl.when(jnp.logical_not(alone))
    def _():
        send_col(m)

    for o in range(FAN, n_col):
        send_row(((first_group + groups - o // FAN) % groups) * FAN + (k + o) % FAN)

    def relay(g, half):
        block = rows_at(col_v, (g * 2 + half) * FAN * BLOCK, FAN * BLOCK)
        return pltpu.make_async_remote_copy(
            src_ref=block, dst_ref=block,
            send_sem=relay_send.at[g], recv_sem=relay_recv.at[g],
            device_id=(sibling, k), device_id_type=MESH,
        )

    def pass_on(g):
        block = rows_at(col_v, (g * 2 + h) * FAN * BLOCK, FAN * BLOCK)
        pltpu.make_async_copy(block, block, c_recv.at[g]).wait()
        relay(g, h).start()

    def exchange(g):
        return pltpu.make_async_remote_copy(
            src_ref=rows_at(cmsg_v, (g * 2 + 1 - h) * FAN * SLOT, FAN * SLOT),
            dst_ref=rows_at(sib_v, g * FAN * SLOT, FAN * SLOT),
            send_sem=sib_send.at[g], recv_sem=sib_recv.at[g],
            device_id=(sibling, k), device_id_type=MESH,
        )

    def row_out(c):
        return pltpu.make_async_remote_copy(
            src_ref=rows_at(rmsg_v, c * SLOT, USED), dst_ref=rows_at(rin_v, k * SLOT, USED),
            send_sem=ro_send.at[c], recv_sem=ro_recv.at[k],
            device_id=(i, c), device_id_type=MESH,
        )

    def cmsg_row(c):
        return (((c // FAN) * 2 + h) * FAN + c % FAN) * SLOT

    def col_out(c):
        return pltpu.make_async_remote_copy(
            src_ref=rows_at(cmsg_v, cmsg_row(c), USED), dst_ref=rows_at(mid_v, k * SLOT, USED),
            send_sem=co_send.at[c], recv_sem=mid_recv.at[k],
            device_id=(i, c), device_id_type=MESH,
        )

    def col_on(source):
        return pltpu.make_async_remote_copy(
            src_ref=rows_at(mid_v, source * SLOT, USED), dst_ref=rows_at(cin_v, m * SLOT, USED),
            send_sem=on_send.at[source], recv_sem=cin_recv.at[m],
            device_id=(2 * source + h, k), device_id_type=MESH,
        )

    def col_direct(c):
        return pltpu.make_async_remote_copy(
            src_ref=rows_at(cmsg_v, cmsg_row(c), USED), dst_ref=rows_at(cin_v, m * SLOT, USED),
            send_sem=co_send.at[c], recv_sem=cin_recv.at[m],
            device_id=(2 * k + h, c), device_id_type=MESH,
        )

    def send_cols(g, last):
        exchange(g).wait_recv()
        base = pl.multiple_of((g * 2 + h) * FAN * SLOT, 8)
        span = pl.ds(base, FAN * SLOT)
        cmsg_v[span] = cmsg_v[span] + sib_v[pl.ds(pl.multiple_of(g * FAN * SLOT, 8), FAN * SLOT)]

        for o in range(FAN):
            c = g * FAN + o
            stays = jnp.logical_and(alone, c == k) if last else c == k
            target, place, sems = (cin_v, m, cin_recv) if last else (mid_v, k, mid_recv)

            @pl.when(stays)
            def _():
                pltpu.make_async_copy(
                    rows_at(cmsg_v, cmsg_row(c), USED), rows_at(target, place * SLOT, USED),
                    sems.at[place],
                ).start()

            @pl.when(jnp.logical_not(stays))
            def _():
                (col_direct if last else col_out)(c).start()

    def send_on(t):
        for o in range(FAN):
            source = ((first_group + groups - t) % groups) * FAN + o
            at = rows_at(mid_v, source * SLOT, USED)
            pltpu.make_async_copy(at, at, mid_recv.at[source]).wait()

            @pl.when(source == m)
            def _():
                pltpu.make_async_copy(
                    rows_at(mid_v, m * SLOT, USED), rows_at(cin_v, m * SLOT, USED), cin_recv.at[m]
                ).start()

            @pl.when(source != m)
            def _():
                col_on(source).start()

    row_of = lax.broadcasted_iota(jnp.int32, (8, LANES), 0)
    lane_of = lax.broadcasted_iota(jnp.int32, (8, LANES), 1)
    block_of = lane_of // 16
    low_row = lax.broadcasted_iota(jnp.int32, (16, LANES), 0)
    low_lane = lax.broadcasted_iota(jnp.int32, (16, LANES), 1)
    widen = jnp.where(
        jnp.logical_and(low_lane // QUOTA == low_row % FAN, low_row < 3 * FAN), 1.0, 0.0
    ).astype(bf16)
    sum_row = lax.broadcasted_iota(jnp.int32, (8, 2 * LANES), 0)
    sum_lane = lax.broadcasted_iota(jnp.int32, (8, 2 * LANES), 1)
    gather = jnp.where((sum_lane % LANES) // QUOTA == sum_row, 1.0, 0.0).astype(bf16)

    part_v[3 * FAN * BLOCK :] = jnp.zeros((FAN * BLOCK, LANES), f32)

    pass_on(first_group)

    @pl.loop(0, groups)
    def _(t):
        g = (first_group + t) % groups

        @pl.when(t + 1 < groups)
        def _():
            pass_on((first_group + t + 1) % groups)

        relay(g, 1 - h).wait_recv()
        block = rows_at(row_v, g * FAN * BLOCK, FAN * BLOCK)
        pltpu.make_async_copy(block, block, r_recv.at[g]).wait()

        for r in range(BLOCK):
            x = col_v[pl.ds(g * (2 * FAN * BLOCK) + r, 8, stride=BLOCK), :]
            for row_bit, lane_bit in SWAPS:
                x = swap_bits(x, row_bit, lane_bit, row_of, block_of)
            right_v[8 * r : 8 * r + 8, :] = x

        value = row_v[pl.ds(pl.multiple_of(g * FAN * BLOCK, 8), FAN * BLOCK), :]
        high = value.astype(bf16).astype(f32)
        rest = value - high
        middle = rest.astype(bf16).astype(f32)
        part_v[0 : FAN * BLOCK] = high
        part_v[FAN * BLOCK : 2 * FAN * BLOCK] = middle
        part_v[2 * FAN * BLOCK : 3 * FAN * BLOCK] = rest - middle
        left_v[...] = jnp.dot(
            jnp.concatenate(
                [part_v[pl.ds(r, 16, stride=BLOCK), :].T for r in range(BLOCK)], axis=0
            ).astype(bf16),
            widen,
            preferred_element_type=f32,
        )

        @pl.when(t == 0)
        def _():
            seen_copy.wait()
            flag_copy.wait()

        sky_copy(g).wait()

        def right_of(d):
            at = (d // 8) * 8 + place_of(d % 8)
            return [
                jnp.broadcast_to(right_v[pl.ds(plane * n_dir + at, 1), :], (8, LANES))
                for plane in range(8)
            ]

        def model_step(n, total):
            for o in range(MODEL_UNROLL):
                d = n * MODEL_UNROLL + o
                right = right_of(d)
                sky = [sky_v[g, plane, d].astype(f32) for plane in range(8)]
                new = []
                for half in range(2):
                    part = [plane[8 * half : 8 * half + 8] for plane in sky]
                    left = [
                        left_v[pl.ds(pl.multiple_of((plane * n_dir + d) * n_p + 8 * half, 8), 8), :]
                        for plane in range(8)
                    ]
                    front = mul(left, part)
                    for plane in range(8):
                        front_v[plane, d, 8 * half : 8 * half + 8] = front[plane]
                        wide_sky_v[plane, d, 8 * half : 8 * half + 8] = part[plane]
                    new += mul_herm(front, right, total[8 * half : 8 * half + 8])
                total = tuple(new)
            return total

        zero = jnp.zeros((8, LANES), f32)
        model = lax.fori_loop(0, n_dir // MODEL_UNROLL, model_step, (zero,) * 16)

        @pl.when(t > 0)
        def _():
            send_cols((first_group + t + groups - 1) % groups, False)

        lanes = lanes_of(g)
        weight, error = [], []
        for half in range(2):
            rows = i * n_p + 8 * half + row_of
            columns = k * QUOTA + lane_of % QUOTA
            kept = flag_v[8 * half : 8 * half + 8, lanes].astype(f32)
            kept = kept * (rows != columns).astype(f32)
            weight.append(kept)
            for plane in range(8):
                seen = seen_v[plane, 8 * half : 8 * half + 8, lanes]
                value = kept * (seen - model[8 * half + plane])
                error.append(value)
                res_v[plane, 8 * half : 8 * half + 8, lanes] = value
        pltpu.make_async_copy(
            res_v.at[:, :, lanes], res_out.at[:, :, lanes], out_sem.at[g]
        ).start()

        def sum_step(n, carry):
            for o in range(SUM_UNROLL):
                d = n * SUM_UNROLL + o
                right = right_of(d)
                rows, cols = [], None
                for half in range(2):
                    wrong = error[8 * half : 8 * half + 8]
                    sky = [wide_sky_v[plane, d, 8 * half : 8 * half + 8] for plane in range(8)]
                    front = [front_v[plane, d, 8 * half : 8 * half + 8] for plane in range(8)]
                    behind = mul_herm(sky, right)
                    rows.append(mul_herm(wrong, behind) + [weight[half] * squares(behind)])
                    col = herm_mul(wrong, front) + [weight[half] * squares(front)]
                    cols = col if cols is None else [a + b for a, b in zip(cols, col)]
                at = pl.ds(pl.multiple_of(d * n_p, 16), n_p)
                for plane in range(9):
                    x = jnp.concatenate([rows[0][plane], rows[1][plane]], axis=0)
                    high = x.astype(bf16)
                    prod_v[plane, at, 0:LANES] = high
                    prod_v[plane, at, LANES : 2 * LANES] = (x - high.astype(f32)).astype(bf16)
                    colsum_v[plane, d] = cols[plane]
            return carry

        lax.fori_loop(0, n_dir // SUM_UNROLL, sum_step, 0)

        for plane in range(9):
            for high in range(n_dir // 8):
                items = [None] * 8
                for low in range(8):
                    items[place_of(low)] = colsum_v[plane, 8 * high + low]
                for bit in range(3):
                    up = ((row_of >> bit) & 1) == 1
                    items = [
                        jnp.where(up, b, a) + pltpu.roll(jnp.where(up, a, b), 1 << bit, 0)
                        for a, b in zip(items[0::2], items[1::2])
                    ]
                x = items[0]
                for row_bit, lane_bit in SWAPS:
                    x = swap_bits(x, row_bit, lane_bit, row_of, block_of)
                cmsg_v[pl.ds(g * 2 * FAN * SLOT + 2 * plane + high, 8, stride=SLOT), :] = x
        exchange(g).start()

        for plane in range(9):
            x = lax.dot_general(
                gather, prod_v[plane], (((1,), (1,)), ((), ())), preferred_element_type=f32
            )
            for high in range(n_dir // 8):
                rmsg_v[pl.ds(g * FAN * SLOT + 2 * plane + high, FAN, stride=SLOT), :] = x[
                    0:FAN, high * LANES : (high + 1) * LANES
                ]

        for o in range(FAN):
            c = g * FAN + o

            @pl.when(c == k)
            def _():
                pltpu.make_async_copy(
                    rows_at(rmsg_v, k * SLOT, USED), rows_at(rin_v, k * SLOT, USED), ro_recv.at[k]
                ).start()

            @pl.when(c != k)
            def _():
                row_out(c).start()

        @pl.when(jnp.logical_and(t > 1, t < groups - 1))
        def _():
            send_on(t - 2)

    last_group = (first_group + groups - 1) % groups
    send_cols(last_group, True)
    for t in range(max(groups - 3, 0), groups - 1):
        send_on(t)

    def add_up(buffer, sems, source, total):
        at = rows_at(buffer, source * SLOT, USED)
        pltpu.make_async_copy(at, at, sems.at[source]).wait()
        start = pl.multiple_of(source * SLOT, 8)
        return tuple(
            part + buffer[pl.ds(start + 8 * n, size), :]
            for n, (part, size) in enumerate(zip(total, (8, 8, 2)))
        )

    def add_step(o, total):
        total = add_up(rin_v, ro_recv, (k + o) % n_col, total)
        return add_up(cin_v, cin_recv, (m + o) % n_col, total)

    zero = jnp.zeros((8, LANES), f32)
    top, bottom, curvature = lax.fori_loop(
        0, n_col, add_step, (zero, zero, jnp.zeros((2, LANES), f32))
    )
    divisor = jnp.where(
        row_of % 2 == 0,
        jnp.broadcast_to(curvature[0:1], (8, LANES)),
        jnp.broadcast_to(curvature[1:2], (8, LANES)),
    ) + epsilon
    fresh = send_v[...] + jnp.concatenate([top / divisor, bottom / divisor], axis=0)
    for j in range(8):
        wide_v[pl.ds(j, BLOCK, stride=8), :] = fresh if j == 0 else pltpu.roll(fresh, LANES - 16 * j, 1)
    new_v[...] = wide_v[:, 0:16]
    new_copy = pltpu.make_async_copy(new_v, gain_out, out_sem.at[groups])
    new_copy.start()

    sent = rows_at(row_v, 0, (n_col - 1) * BLOCK)
    pltpu.make_async_copy(sent, sent, r_send.at[0]).wait()

    @pl.when(alone)
    def _():
        sent = rows_at(row_v, 0, (n_col - 1) * BLOCK)
        pltpu.make_async_copy(sent, sent, c_send.at[0]).wait()

    @pl.when(jnp.logical_not(alone))
    def _():
        sent = rows_at(row_v, 0, n_col * BLOCK)
        pltpu.make_async_copy(sent, sent, c_send.at[0]).wait()

    @pl.loop(0, groups)
    def _(g):
        relay(g, h).wait_send()
        exchange(g).wait_send()
        lanes = lanes_of(g)
        pltpu.make_async_copy(
            res_v.at[:, :, lanes], res_out.at[:, :, lanes], out_sem.at[g]
        ).wait()

    @pl.loop(0, n_col)
    def _(c):
        @pl.when(c != k)
        def _():
            row_out(c).wait_send()

        last = c // FAN == last_group
        stays = jnp.where(last, jnp.where(alone, c, -1), c) == k

        @pl.when(jnp.logical_not(stays))
        def _():
            col_direct(c).wait_send()

        late = (c // FAN + groups - 1) % groups == first_group

        @pl.when(jnp.logical_not(jnp.logical_or(late, c == m)))
        def _():
            col_on(c).wait_send()

    new_copy.wait()


def on_device(coherency, visibilities, flags, gains):
    n_col = lax.axis_size("col")
    n_dir, n_p, width = coherency.shape[1], coherency.shape[4], coherency.shape[5]
    groups = width // LANES
    sky = coherency.reshape(8, n_dir, n_p, width)
    seen = visibilities.reshape(8, n_p, width)
    flag = flags.reshape(n_p, width)
    mine = gains.reshape(8 * n_dir, n_p)
    f32, bf16 = jnp.float32, jnp.bfloat16
    any_spec = pl.BlockSpec(memory_space=pl.ANY)
    dma = pltpu.SemaphoreType.DMA
    residual, fresh = pl.pallas_call(
        functools.partial(kernel, n_col, n_dir, n_p),
        out_shape=(
            jax.ShapeDtypeStruct(seen.shape, f32),
            jax.ShapeDtypeStruct(mine.shape, f32),
        ),
        in_specs=[any_spec] * 4,
        out_specs=(any_spec, any_spec),
        scratch_shapes=[
            pltpu.VMEM((groups, 8, n_dir, n_p, LANES), bf16),
            pltpu.VMEM(seen.shape, f32),
            pltpu.VMEM(flag.shape, jnp.int32),
            pltpu.VMEM(mine.shape, f32),
            pltpu.VMEM((8 * n_dir, LANES), f32),
            pltpu.VMEM((BLOCK, LANES), f32),
            pltpu.VMEM((n_col * BLOCK, LANES), f32),
            pltpu.VMEM((2 * n_col * BLOCK, LANES), f32),
            pltpu.VMEM((4 * FAN * BLOCK, LANES), f32),
            pltpu.VMEM((8 * n_dir * n_p, LANES), f32),
            pltpu.VMEM((8 * n_dir, LANES), f32),
            pltpu.VMEM((8, n_dir, n_p, LANES), f32),
            pltpu.VMEM((8, n_dir, n_p, LANES), f32),
            pltpu.VMEM(seen.shape, f32),
            pltpu.VMEM((9, n_dir * n_p, 2 * LANES), bf16),
            pltpu.VMEM((9, n_dir, 8, LANES), f32),
            pltpu.VMEM((n_col * SLOT, LANES), f32),
            pltpu.VMEM((2 * n_col * SLOT, LANES), f32),
            pltpu.VMEM((n_col * SLOT, LANES), f32),
            pltpu.VMEM((n_col * SLOT, LANES), f32),
            pltpu.VMEM((n_col * SLOT, LANES), f32),
            pltpu.VMEM((n_col * SLOT, LANES), f32),
            pltpu.VMEM(mine.shape, f32),
            dma((3 + groups,)),
            dma((1,)),
            dma((1,)),
            dma((groups,)),
            dma((groups,)),
            dma((groups,)),
            dma((groups,)),
            dma((groups,)),
            dma((groups,)),
            dma((n_col,)),
            dma((n_col,)),
            dma((n_col,)),
            dma((n_col,)),
            dma((n_col,)),
            dma((n_col,)),
            dma((groups + 1,)),
        ],
        compiler_params=pltpu.CompilerParams(
            collective_id=0, has_side_effects=True, vmem_limit_bytes=56 * 1024 * 1024
        ),
    )(sky, seen, flag, mine)
    return residual.reshape(visibilities.shape), fresh.reshape(gains.shape)


def solution(mesh):
    return jax.shard_map(
        on_device,
        mesh=mesh,
        in_specs=(
            P(None, None, None, "col", "row", None),
            P(None, None, "col", "row", None),
            P(None, "col", "row", None),
            P(None, None, "col", "row"),
        ),
        out_specs=(P(None, None, "col", "row", None), P(None, None, "col", "row")),
        check_vma=False,
    )
```

```python
import functools

import jax
import jax.numpy as jnp
from jax import lax
from jax.experimental import pallas as pl
from jax.experimental.pallas import tpu as pltpu
from jax.sharding import PartitionSpec as P

epsilon = 1e-06
MESH = pl.DeviceIdType.MESH
LANES = 128
QUOTA = 32
FAN = LANES // QUOTA
SLOT = 24
MODEL_UNROLL = 8
SUM_UNROLL = 8
USED = 18
BLOCK = 16


def mul(first, second):
    out = []
    for a in range(2):
        for b in range(2):
            re = im = None
            for k in range(2):
                fr, fi = first[4 * a + 2 * k], first[4 * a + 2 * k + 1]
                sr, si = second[4 * k + 2 * b], second[4 * k + 2 * b + 1]
                r, i = fr * sr - fi * si, fr * si + fi * sr
                re, im = (r, i) if re is None else (re + r, im + i)
            out += [re, im]
    return out


def mul_herm(first, second, total=None):
    out = []
    for a in range(2):
        for c in range(2):
            re = im = None
            if total is not None:
                re, im = total[4 * a + 2 * c], total[4 * a + 2 * c + 1]
            for b in range(2):
                fr, fi = first[4 * a + 2 * b], first[4 * a + 2 * b + 1]
                sr, si = second[4 * c + 2 * b], second[4 * c + 2 * b + 1]
                r, i = fr * sr + fi * si, fi * sr - fr * si
                re, im = (r, i) if re is None else (re + r, im + i)
            out += [re, im]
    return out


def herm_mul(first, second):
    out = []
    for a in range(2):
        for c in range(2):
            re = im = None
            for b in range(2):
                fr, fi = first[4 * b + 2 * a], first[4 * b + 2 * a + 1]
                sr, si = second[4 * b + 2 * c], second[4 * b + 2 * c + 1]
                r, i = sr * fr + si * fi, si * fr - sr * fi
                re, im = (r, i) if re is None else (re + r, im + i)
            out += [re, im]
    return out


def squares(planes):
    total = planes[0] * planes[0]
    for plane in planes[1:]:
        total = total + plane * plane
    return total


def swap_bits(x, row_bit, lane_bit, row_of, block_of):
    row_high = (row_of >> row_bit) & 1
    lane_high = (block_of >> lane_bit) & 1
    rows, lanes = 1 << row_bit, 16 << lane_bit
    up = pltpu.roll(pltpu.roll(x, 8 - rows, 0), lanes, 1)
    down = pltpu.roll(pltpu.roll(x, rows, 0), LANES - lanes, 1)
    return jnp.where(row_high == lane_high, x, jnp.where(row_high == 0, up, down))


def place_of(low):
    return (low % 2) * 4 + ((low // 4) % 2) * 2 + (low // 2) % 2


SWAPS = ((2, 0), (1, 2), (0, 1))


def kernel(
    n_col, n_dir, n_p,
    sky_ref, seen_ref, flag_ref, gain_ref, res_out, gain_out,
    sky_v, seen_v, flag_v, gain_v, wide_v, send_v, row_v, col_v, part_v, left_v, right_v,
    front_v, wide_sky_v, res_v, prod_v, colsum_v, rmsg_v, cmsg_v, sib_v, rin_v, mid_v, cin_v, new_v,
    in_sem, r_send, c_send, r_recv, c_recv, relay_send, relay_recv, sib_send, sib_recv,
    ro_send, ro_recv, co_send, mid_recv, on_send, cin_recv, out_sem,
):
    i, k = lax.axis_index("row"), lax.axis_index("col")
    m, h = i // 2, i % 2
    groups = n_col // FAN
    first_group = k // FAN
    sibling = 2 * m + (1 - h)
    alone = k == m
    f32, bf16 = jnp.float32, jnp.bfloat16

    def lanes_of(g):
        return pl.ds(pl.multiple_of(g * LANES, LANES), LANES)

    def rows_at(ref, start, size):
        return ref.at[pl.ds(pl.multiple_of(start, 8), size)]

    gain_copy = pltpu.make_async_copy(gain_ref, gain_v, in_sem.at[0])
    gain_copy.start()
    seen_copy = pltpu.make_async_copy(seen_ref, seen_v, in_sem.at[1])
    flag_copy = pltpu.make_async_copy(flag_ref, flag_v, in_sem.at[2])

    def sky_copy(g):
        return pltpu.make_async_copy(
            sky_ref.at[:, :, :, lanes_of(g)], sky_v.at[g], in_sem.at[3 + g]
        )

    barrier = pltpu.get_barrier_semaphore()

    def signal(row, col):
        pl.semaphore_signal(barrier, inc=1, device_id=(row, col), device_id_type=MESH)

    signal(sibling, k)

    @pl.loop(1, n_col)
    def _(o):
        signal(i, (k + o) % n_col)

    @pl.loop(0, n_col)
    def _(o):
        c = (m + o) % n_col

        @pl.when(jnp.logical_not(jnp.logical_and(alone, c == m)))
        def _():
            signal(2 * k + h, c)

    for t in range(groups):
        sky_copy((first_group + t) % groups).start()
    seen_copy.start()
    flag_copy.start()

    gain_copy.wait()
    wide_v[...] = jnp.zeros_like(wide_v)
    wide_v[:, 0:16] = gain_v[...]
    own = wide_v[pl.ds(0, BLOCK, stride=8), :]
    for j in range(1, 8):
        own = own + pltpu.roll(wide_v[pl.ds(j, BLOCK, stride=8), :], 16 * j, 1)
    send_v[...] = own

    pl.semaphore_wait(barrier, 2 * n_col - alone.astype(jnp.int32))

    def col_row(c, half):
        return (((c // FAN) * 2 + half) * FAN + c % FAN) * BLOCK

    def send_row(c):
        pltpu.make_async_remote_copy(
            src_ref=send_v, dst_ref=rows_at(row_v, k * BLOCK, BLOCK),
            send_sem=r_send.at[0], recv_sem=r_recv.at[k // FAN],
            device_id=(i, c), device_id_type=MESH,
        ).start()

    def send_col(target):
        pltpu.make_async_remote_copy(
            src_ref=send_v, dst_ref=rows_at(col_v, col_row(k, h), BLOCK),
            send_sem=c_send.at[0], recv_sem=c_recv.at[k // FAN],
            device_id=(2 * target + h, m), device_id_type=MESH,
        ).start()

    pltpu.make_async_copy(
        send_v, rows_at(row_v, k * BLOCK, BLOCK), r_recv.at[k // FAN]
    ).start()

    @pl.when(alone)
    def _():
        pltpu.make_async_copy(
            send_v, rows_at(col_v, col_row(k, h), BLOCK), c_recv.at[k // FAN]
        ).start()

    for o in range(1, n_col):
        send_col((m + o) % n_col)

    @pl.when(jnp.logical_not(alone))
    def _():
        send_col(m)

    for o in range(1, FAN):
        send_row(first_group * FAN + (k + o) % FAN)

    for o in range(FAN, n_col):
        send_row(((first_group + groups - o // FAN) % groups) * FAN + (k + o) % FAN)

    def relay(g, half):
        block = rows_at(col_v, (g * 2 + half) * FAN * BLOCK, FAN * BLOCK)
        return pltpu.make_async_remote_copy(
            src_ref=block, dst_ref=block,
            send_sem=relay_send.at[g], recv_sem=relay_recv.at[g],
            device_id=(sibling, k), device_id_type=MESH,
        )

    def pass_on(g):
        block = rows_at(col_v, (g * 2 + h) * FAN * BLOCK, FAN * BLOCK)
        pltpu.make_async_copy(block, block, c_recv.at[g]).wait()
        relay(g, h).start()

    def exchange(g):
        return pltpu.make_async_remote_copy(
            src_ref=rows_at(cmsg_v, (g * 2 + 1 - h) * FAN * SLOT, FAN * SLOT),
            dst_ref=rows_at(sib_v, g * FAN * SLOT, FAN * SLOT),
            send_sem=sib_send.at[g], recv_sem=sib_recv.at[g],
            device_id=(sibling, k), device_id_type=MESH,
        )

    def row_out(c):
        return pltpu.make_async_remote_copy(
            src_ref=rows_at(rmsg_v, c * SLOT, USED), dst_ref=rows_at(rin_v, k * SLOT, USED),
            send_sem=ro_send.at[c], recv_sem=ro_recv.at[k],
            device_id=(i, c), device_id_type=MESH,
        )

    def cmsg_row(c):
        return (((c // FAN) * 2 + h) * FAN + c % FAN) * SLOT

    def col_out(c):
        return pltpu.make_async_remote_copy(
            src_ref=rows_at(cmsg_v, cmsg_row(c), USED), dst_ref=rows_at(mid_v, k * SLOT, USED),
            send_sem=co_send.at[c], recv_sem=mid_recv.at[k],
            device_id=(i, c), device_id_type=MESH,
        )

    def col_on(source):
        return pltpu.make_async_remote_copy(
            src_ref=rows_at(mid_v, source * SLOT, USED), dst_ref=rows_at(cin_v, m * SLOT, USED),
            send_sem=on_send.at[source], recv_sem=cin_recv.at[m],
            device_id=(2 * source + h, k), device_id_type=MESH,
        )

    def col_direct(c):
        return pltpu.make_async_remote_copy(
            src_ref=rows_at(cmsg_v, cmsg_row(c), USED), dst_ref=rows_at(cin_v, m * SLOT, USED),
            send_sem=co_send.at[c], recv_sem=cin_recv.at[m],
            device_id=(2 * k + h, c), device_id_type=MESH,
        )

    def send_cols(g, last):
        exchange(g).wait_recv()
        base = pl.multiple_of((g * 2 + h) * FAN * SLOT, 8)
        span = pl.ds(base, FAN * SLOT)
        cmsg_v[span] = cmsg_v[span] + sib_v[pl.ds(pl.multiple_of(g * FAN * SLOT, 8), FAN * SLOT)]

        for o in range(FAN):
            c = g * FAN + o
            stays = jnp.logical_and(alone, c == k) if last else c == k
            target, place, sems = (cin_v, m, cin_recv) if last else (mid_v, k, mid_recv)

            @pl.when(stays)
            def _():
                pltpu.make_async_copy(
                    rows_at(cmsg_v, cmsg_row(c), USED), rows_at(target, place * SLOT, USED),
                    sems.at[place],
                ).start()

            @pl.when(jnp.logical_not(stays))
            def _():
                (col_direct if last else col_out)(c).start()

    def send_on(t):
        for o in range(FAN):
            source = ((first_group + groups - t) % groups) * FAN + o
            at = rows_at(mid_v, source * SLOT, USED)
            pltpu.make_async_copy(at, at, mid_recv.at[source]).wait()

            @pl.when(source == m)
            def _():
                pltpu.make_async_copy(
                    rows_at(mid_v, m * SLOT, USED), rows_at(cin_v, m * SLOT, USED), cin_recv.at[m]
                ).start()

            @pl.when(source != m)
            def _():
                col_on(source).start()

    row_of = lax.broadcasted_iota(jnp.int32, (8, LANES), 0)
    lane_of = lax.broadcasted_iota(jnp.int32, (8, LANES), 1)
    block_of = lane_of // 16
    low_row = lax.broadcasted_iota(jnp.int32, (16, LANES), 0)
    low_lane = lax.broadcasted_iota(jnp.int32, (16, LANES), 1)
    widen = jnp.where(
        jnp.logical_and(low_lane // QUOTA == low_row % FAN, low_row < 3 * FAN), 1.0, 0.0
    ).astype(bf16)
    sum_row = lax.broadcasted_iota(jnp.int32, (8, 2 * LANES), 0)
    sum_lane = lax.broadcasted_iota(jnp.int32, (8, 2 * LANES), 1)
    gather = jnp.where((sum_lane % LANES) // QUOTA == sum_row, 1.0, 0.0).astype(bf16)

    part_v[3 * FAN * BLOCK :] = jnp.zeros((FAN * BLOCK, LANES), f32)

    pass_on(first_group)

    @pl.loop(0, groups)
    def _(t):
        g = (first_group + t) % groups

        @pl.when(t + 1 < groups)
        def _():
            pass_on((first_group + t + 1) % groups)

        relay(g, 1 - h).wait_recv()
        block = rows_at(row_v, g * FAN * BLOCK, FAN * BLOCK)
        pltpu.make_async_copy(block, block, r_recv.at[g]).wait()

        for r in range(BLOCK):
            x = col_v[pl.ds(g * (2 * FAN * BLOCK) + r, 8, stride=BLOCK), :]
            for row_bit, lane_bit in SWAPS:
                x = swap_bits(x, row_bit, lane_bit, row_of, block_of)
            right_v[8 * r : 8 * r + 8, :] = x

        value = row_v[pl.ds(pl.multiple_of(g * FAN * BLOCK, 8), FAN * BLOCK), :]
        high = value.astype(bf16).astype(f32)
        rest = value - high
        middle = rest.astype(bf16).astype(f32)
        part_v[0 : FAN * BLOCK] = high
        part_v[FAN * BLOCK : 2 * FAN * BLOCK] = middle
        part_v[2 * FAN * BLOCK : 3 * FAN * BLOCK] = rest - middle
        left_v[...] = jnp.dot(
            jnp.concatenate(
                [part_v[pl.ds(r, 16, stride=BLOCK), :].T for r in range(BLOCK)], axis=0
            ).astype(bf16),
            widen,
            preferred_element_type=f32,
        )

        @pl.when(t == 0)
        def _():
            seen_copy.wait()
            flag_copy.wait()

        sky_copy(g).wait()

        def right_of(d):
            at = (d // 8) * 8 + place_of(d % 8)
            return [
                jnp.broadcast_to(right_v[pl.ds(plane * n_dir + at, 1), :], (8, LANES))
                for plane in range(8)
            ]

        def model_step(n, total):
            for o in range(MODEL_UNROLL):
                d = n * MODEL_UNROLL + o
                right = right_of(d)
                sky = [sky_v[g, plane, d].astype(f32) for plane in range(8)]
                new = []
                for half in range(2):
                    part = [plane[8 * half : 8 * half + 8] for plane in sky]
                    left = [
                        left_v[pl.ds(pl.multiple_of((plane * n_dir + d) * n_p + 8 * half, 8), 8), :]
                        for plane in range(8)
                    ]
                    front = mul(left, part)
                    for plane in range(8):
                        front_v[plane, d, 8 * half : 8 * half + 8] = front[plane]
                        wide_sky_v[plane, d, 8 * half : 8 * half + 8] = part[plane]
                    new += mul_herm(front, right, total[8 * half : 8 * half + 8])
                total = tuple(new)
            return total

        zero = jnp.zeros((8, LANES), f32)
        model = lax.fori_loop(0, n_dir // MODEL_UNROLL, model_step, (zero,) * 16)

        @pl.when(t > 0)
        def _():
            send_cols((first_group + t + groups - 1) % groups, False)

        lanes = lanes_of(g)
        weight, error = [], []
        for half in range(2):
            rows = i * n_p + 8 * half + row_of
            columns = k * QUOTA + lane_of % QUOTA
            kept = flag_v[8 * half : 8 * half + 8, lanes].astype(f32)
            kept = kept * (rows != columns).astype(f32)
            weight.append(kept)
            for plane in range(8):
                seen = seen_v[plane, 8 * half : 8 * half + 8, lanes]
                value = kept * (seen - model[8 * half + plane])
                error.append(value)
                res_v[plane, 8 * half : 8 * half + 8, lanes] = value
        pltpu.make_async_copy(
            res_v.at[:, :, lanes], res_out.at[:, :, lanes], out_sem.at[g]
        ).start()

        def sum_step(n, carry):
            for o in range(SUM_UNROLL):
                d = n * SUM_UNROLL + o
                right = right_of(d)
                rows, cols = [], None
                for half in range(2):
                    wrong = error[8 * half : 8 * half + 8]
                    sky = [wide_sky_v[plane, d, 8 * half : 8 * half + 8] for plane in range(8)]
                    front = [front_v[plane, d, 8 * half : 8 * half + 8] for plane in range(8)]
                    behind = mul_herm(sky, right)
                    rows.append(mul_herm(wrong, behind) + [weight[half] * squares(behind)])
                    col = herm_mul(wrong, front) + [weight[half] * squares(front)]
                    cols = col if cols is None else [a + b for a, b in zip(cols, col)]
                at = pl.ds(pl.multiple_of(d * n_p, 16), n_p)
                for plane in range(9):
                    x = jnp.concatenate([rows[0][plane], rows[1][plane]], axis=0)
                    high = x.astype(bf16)
                    prod_v[plane, at, 0:LANES] = high
                    prod_v[plane, at, LANES : 2 * LANES] = (x - high.astype(f32)).astype(bf16)
                    colsum_v[plane, d] = cols[plane]
            return carry

        lax.fori_loop(0, n_dir // SUM_UNROLL, sum_step, 0)

        for plane in range(9):
            for high in range(n_dir // 8):
                items = [None] * 8
                for low in range(8):
                    items[place_of(low)] = colsum_v[plane, 8 * high + low]
                for bit in range(3):
                    up = ((row_of >> bit) & 1) == 1
                    items = [
                        jnp.where(up, b, a) + pltpu.roll(jnp.where(up, a, b), 1 << bit, 0)
                        for a, b in zip(items[0::2], items[1::2])
                    ]
                x = items[0]
                for row_bit, lane_bit in SWAPS:
                    x = swap_bits(x, row_bit, lane_bit, row_of, block_of)
                cmsg_v[pl.ds(g * 2 * FAN * SLOT + 2 * plane + high, 8, stride=SLOT), :] = x
        exchange(g).start()

        for plane in range(9):
            x = lax.dot_general(
                gather, prod_v[plane], (((1,), (1,)), ((), ())), preferred_element_type=f32
            )
            for high in range(n_dir // 8):
                rmsg_v[pl.ds(g * FAN * SLOT + 2 * plane + high, FAN, stride=SLOT), :] = x[
                    0:FAN, high * LANES : (high + 1) * LANES
                ]

        for o in range(FAN):
            c = g * FAN + o

            @pl.when(c == k)
            def _():
                pltpu.make_async_copy(
                    rows_at(rmsg_v, k * SLOT, USED), rows_at(rin_v, k * SLOT, USED), ro_recv.at[k]
                ).start()

            @pl.when(c != k)
            def _():
                row_out(c).start()

        @pl.when(t > 1)
        def _():
            send_on(t - 2)

    last_group = (first_group + groups - 1) % groups
    send_cols(last_group, True)
    for t in range(max(groups - 2, 0), groups - 1):
        send_on(t)

    def add_up(buffer, sems, source, total):
        at = rows_at(buffer, source * SLOT, USED)
        pltpu.make_async_copy(at, at, sems.at[source]).wait()
        start = pl.multiple_of(source * SLOT, 8)
        return tuple(
            part + buffer[pl.ds(start + 8 * n, size), :]
            for n, (part, size) in enumerate(zip(total, (8, 8, 2)))
        )

    def add_step(o, total):
        total = add_up(rin_v, ro_recv, (k + o) % n_col, total)
        return add_up(cin_v, cin_recv, (m + o) % n_col, total)

    zero = jnp.zeros((8, LANES), f32)
    top, bottom, curvature = lax.fori_loop(
        0, n_col, add_step, (zero, zero, jnp.zeros((2, LANES), f32))
    )
    divisor = jnp.where(
        row_of % 2 == 0,
        jnp.broadcast_to(curvature[0:1], (8, LANES)),
        jnp.broadcast_to(curvature[1:2], (8, LANES)),
    ) + epsilon
    fresh = send_v[...] + jnp.concatenate([top / divisor, bottom / divisor], axis=0)
    for j in range(8):
        wide_v[pl.ds(j, BLOCK, stride=8), :] = fresh if j == 0 else pltpu.roll(fresh, LANES - 16 * j, 1)
    new_v[...] = wide_v[:, 0:16]
    new_copy = pltpu.make_async_copy(new_v, gain_out, out_sem.at[groups])
    new_copy.start()

    sent = rows_at(row_v, 0, (n_col - 1) * BLOCK)
    pltpu.make_async_copy(sent, sent, r_send.at[0]).wait()

    @pl.when(alone)
    def _():
        sent = rows_at(row_v, 0, (n_col - 1) * BLOCK)
        pltpu.make_async_copy(sent, sent, c_send.at[0]).wait()

    @pl.when(jnp.logical_not(alone))
    def _():
        sent = rows_at(row_v, 0, n_col * BLOCK)
        pltpu.make_async_copy(sent, sent, c_send.at[0]).wait()

    @pl.loop(0, groups)
    def _(g):
        relay(g, h).wait_send()
        exchange(g).wait_send()
        lanes = lanes_of(g)
        pltpu.make_async_copy(
            res_v.at[:, :, lanes], res_out.at[:, :, lanes], out_sem.at[g]
        ).wait()

    @pl.loop(0, n_col)
    def _(c):
        @pl.when(c != k)
        def _():
            row_out(c).wait_send()

        last = c // FAN == last_group
        stays = jnp.where(last, jnp.where(alone, c, -1), c) == k

        @pl.when(jnp.logical_not(stays))
        def _():
            col_direct(c).wait_send()

        late = (c // FAN + groups - 1) % groups == first_group

        @pl.when(jnp.logical_not(jnp.logical_or(late, c == m)))
        def _():
            col_on(c).wait_send()

    new_copy.wait()


def hand_over(res_ref, gain_ref, res_out, gain_out, res_v, gain_v, sems):
    pairs = [(gain_ref, gain_v, gain_out)]
    for n in range(0, 8, 2):
        pairs.append((res_ref.at[n : n + 2], res_v.at[n : n + 2], res_out.at[n : n + 2]))
    first = [pltpu.make_async_copy(a, b, sems.at[n]) for n, (a, b, _) in enumerate(pairs)]
    second = [pltpu.make_async_copy(b, c, sems.at[5 + n]) for n, (_, b, c) in enumerate(pairs)]
    for copy in first:
        copy.start()
    for before, after in zip(first, second):
        before.wait()
        after.start()
    for copy in second:
        copy.wait()


def on_device(coherency, visibilities, flags, gains):
    n_col = lax.axis_size("col")
    n_dir, n_p, width = coherency.shape[1], coherency.shape[4], coherency.shape[5]
    groups = width // LANES
    sky = coherency.reshape(8, n_dir, n_p, width)
    seen = visibilities.reshape(8, n_p, width)
    flag = flags.reshape(n_p, width)
    mine = gains.reshape(8 * n_dir, n_p)
    f32, bf16 = jnp.float32, jnp.bfloat16
    any_spec = pl.BlockSpec(memory_space=pl.ANY)
    dma = pltpu.SemaphoreType.DMA
    residual, fresh = pl.pallas_call(
        functools.partial(kernel, n_col, n_dir, n_p),
        out_shape=(
            jax.ShapeDtypeStruct(seen.shape, f32),
            jax.ShapeDtypeStruct(mine.shape, f32),
        ),
        in_specs=[any_spec] * 4,
        out_specs=(any_spec, any_spec),
        scratch_shapes=[
            pltpu.VMEM((groups, 8, n_dir, n_p, LANES), bf16),
            pltpu.VMEM(seen.shape, f32),
            pltpu.VMEM(flag.shape, jnp.int32),
            pltpu.VMEM(mine.shape, f32),
            pltpu.VMEM((8 * n_dir, LANES), f32),
            pltpu.VMEM((BLOCK, LANES), f32),
            pltpu.VMEM((n_col * BLOCK, LANES), f32),
            pltpu.VMEM((2 * n_col * BLOCK, LANES), f32),
            pltpu.VMEM((4 * FAN * BLOCK, LANES), f32),
            pltpu.VMEM((8 * n_dir * n_p, LANES), f32),
            pltpu.VMEM((8 * n_dir, LANES), f32),
            pltpu.VMEM((8, n_dir, n_p, LANES), f32),
            pltpu.VMEM((8, n_dir, n_p, LANES), f32),
            pltpu.VMEM(seen.shape, f32),
            pltpu.VMEM((9, n_dir * n_p, 2 * LANES), bf16),
            pltpu.VMEM((9, n_dir, 8, LANES), f32),
            pltpu.VMEM((n_col * SLOT, LANES), f32),
            pltpu.VMEM((2 * n_col * SLOT, LANES), f32),
            pltpu.VMEM((n_col * SLOT, LANES), f32),
            pltpu.VMEM((n_col * SLOT, LANES), f32),
            pltpu.VMEM((n_col * SLOT, LANES), f32),
            pltpu.VMEM((n_col * SLOT, LANES), f32),
            pltpu.VMEM(mine.shape, f32),
            dma((3 + groups,)),
            dma((1,)),
            dma((1,)),
            dma((groups,)),
            dma((groups,)),
            dma((groups,)),
            dma((groups,)),
            dma((groups,)),
            dma((groups,)),
            dma((n_col,)),
            dma((n_col,)),
            dma((n_col,)),
            dma((n_col,)),
            dma((n_col,)),
            dma((n_col,)),
            dma((groups + 1,)),
        ],
        compiler_params=pltpu.CompilerParams(
            collective_id=0, has_side_effects=True, vmem_limit_bytes=56 * 1024 * 1024
        ),
    )(sky, seen, flag, mine)
    residual, fresh = pl.pallas_call(
        hand_over,
        out_shape=(
            jax.ShapeDtypeStruct(seen.shape, f32),
            jax.ShapeDtypeStruct(mine.shape, f32),
        ),
        in_specs=[any_spec] * 2,
        out_specs=(any_spec, any_spec),
        scratch_shapes=[pltpu.VMEM(seen.shape, f32), pltpu.VMEM(mine.shape, f32), dma((10,))],
        compiler_params=pltpu.CompilerParams(vmem_limit_bytes=56 * 1024 * 1024),
    )(residual, fresh)
    return residual.reshape(visibilities.shape), fresh.reshape(gains.shape)


def solution(mesh):
    return jax.shard_map(
        on_device,
        mesh=mesh,
        in_specs=(
            P(None, None, None, "col", "row", None),
            P(None, None, "col", "row", None),
            P(None, "col", "row", None),
            P(None, None, "col", "row"),
        ),
        out_specs=(P(None, None, "col", "row", None), P(None, None, "col", "row")),
        check_vma=False,
    )
```

```python
import functools

import jax
import jax.numpy as jnp
from jax import lax
from jax.experimental import pallas as pl
from jax.experimental.pallas import tpu as pltpu
from jax.sharding import PartitionSpec as P

epsilon = 1e-06
MESH = pl.DeviceIdType.MESH
LANES = 128
QUOTA = 32
FAN = LANES // QUOTA
SLOT = 24
MODEL_UNROLL = 8
SUM_UNROLL = 8
USED = 18
BLOCK = 16


def mul(first, second):
    out = []
    for a in range(2):
        for b in range(2):
            re = im = None
            for k in range(2):
                fr, fi = first[4 * a + 2 * k], first[4 * a + 2 * k + 1]
                sr, si = second[4 * k + 2 * b], second[4 * k + 2 * b + 1]
                r, i = fr * sr - fi * si, fr * si + fi * sr
                re, im = (r, i) if re is None else (re + r, im + i)
            out += [re, im]
    return out


def mul_herm(first, second, total=None):
    out = []
    for a in range(2):
        for c in range(2):
            re = im = None
            if total is not None:
                re, im = total[4 * a + 2 * c], total[4 * a + 2 * c + 1]
            for b in range(2):
                fr, fi = first[4 * a + 2 * b], first[4 * a + 2 * b + 1]
                sr, si = second[4 * c + 2 * b], second[4 * c + 2 * b + 1]
                r, i = fr * sr + fi * si, fi * sr - fr * si
                re, im = (r, i) if re is None else (re + r, im + i)
            out += [re, im]
    return out


def herm_mul(first, second):
    out = []
    for a in range(2):
        for c in range(2):
            re = im = None
            for b in range(2):
                fr, fi = first[4 * b + 2 * a], first[4 * b + 2 * a + 1]
                sr, si = second[4 * b + 2 * c], second[4 * b + 2 * c + 1]
                r, i = sr * fr + si * fi, si * fr - sr * fi
                re, im = (r, i) if re is None else (re + r, im + i)
            out += [re, im]
    return out


def squares(planes):
    total = planes[0] * planes[0]
    for plane in planes[1:]:
        total = total + plane * plane
    return total


def swap_bits(x, row_bit, lane_bit, row_of, block_of):
    row_high = (row_of >> row_bit) & 1
    lane_high = (block_of >> lane_bit) & 1
    rows, lanes = 1 << row_bit, 16 << lane_bit
    up = pltpu.roll(pltpu.roll(x, 8 - rows, 0), lanes, 1)
    down = pltpu.roll(pltpu.roll(x, rows, 0), LANES - lanes, 1)
    return jnp.where(row_high == lane_high, x, jnp.where(row_high == 0, up, down))


def place_of(low):
    return (low % 2) * 4 + ((low // 4) % 2) * 2 + (low // 2) % 2


SWAPS = ((2, 0), (1, 2), (0, 1))


def kernel(
    n_col, n_dir, n_p,
    sky_ref, seen_ref, flag_ref, gain_ref, res_out, gain_out,
    sky_v, seen_v, flag_v, gain_v, wide_v, send_v, row_v, col_v, part_v, left_v, right_v,
    front_v, wide_sky_v, res_v, prod_v, colsum_v, rmsg_v, cmsg_v, sib_v, rin_v, mid_v, cin_v, new_v,
    in_sem, r_send, c_send, r_recv, c_recv, relay_send, relay_recv, sib_send, sib_recv,
    ro_send, ro_recv, co_send, mid_recv, on_send, cin_recv, out_sem,
):
    i, k = lax.axis_index("row"), lax.axis_index("col")
    m, h = i // 2, i % 2
    groups = n_col // FAN
    first_group = k // FAN
    sibling = 2 * m + (1 - h)
    alone = k == m
    f32, bf16 = jnp.float32, jnp.bfloat16

    def lanes_of(g):
        return pl.ds(pl.multiple_of(g * LANES, LANES), LANES)

    def rows_at(ref, start, size):
        return ref.at[pl.ds(pl.multiple_of(start, 8), size)]

    gain_copy = pltpu.make_async_copy(gain_ref, gain_v, in_sem.at[0])
    gain_copy.start()
    seen_copy = pltpu.make_async_copy(seen_ref, seen_v, in_sem.at[1])
    flag_copy = pltpu.make_async_copy(flag_ref, flag_v, in_sem.at[2])

    def sky_copy(g):
        return pltpu.make_async_copy(
            sky_ref.at[:, :, :, lanes_of(g)], sky_v.at[g], in_sem.at[3 + g]
        )

    barrier = pltpu.get_barrier_semaphore()

    def signal(row, col):
        pl.semaphore_signal(barrier, inc=1, device_id=(row, col), device_id_type=MESH)

    for o in range(1, n_col):
        signal(2 * k + h, (m + o) % n_col)

    @pl.when(jnp.logical_not(alone))
    def _():
        signal(2 * k + h, m)

    for o in range(1, n_col):
        signal(i, (k + o) % n_col)
    signal(sibling, k)

    for t in range(groups):
        sky_copy((first_group + t) % groups).start()
    seen_copy.start()
    flag_copy.start()

    gain_copy.wait()
    wide_v[...] = jnp.zeros_like(wide_v)
    wide_v[:, 0:16] = gain_v[...]
    own = wide_v[pl.ds(0, BLOCK, stride=8), :]
    for j in range(1, 8):
        own = own + pltpu.roll(wide_v[pl.ds(j, BLOCK, stride=8), :], 16 * j, 1)
    send_v[...] = own

    pl.semaphore_wait(barrier, 2 * n_col - alone.astype(jnp.int32))

    def col_row(c, half):
        return (((c // FAN) * 2 + half) * FAN + c % FAN) * BLOCK

    def send_row(c):
        pltpu.make_async_remote_copy(
            src_ref=send_v, dst_ref=rows_at(row_v, k * BLOCK, BLOCK),
            send_sem=r_send.at[0], recv_sem=r_recv.at[k // FAN],
            device_id=(i, c), device_id_type=MESH,
        ).start()

    def send_col(target):
        pltpu.make_async_remote_copy(
            src_ref=send_v, dst_ref=rows_at(col_v, col_row(k, h), BLOCK),
            send_sem=c_send.at[0], recv_sem=c_recv.at[k // FAN],
            device_id=(2 * target + h, m), device_id_type=MESH,
        ).start()

    pltpu.make_async_copy(
        send_v, rows_at(row_v, k * BLOCK, BLOCK), r_recv.at[k // FAN]
    ).start()

    @pl.when(alone)
    def _():
        pltpu.make_async_copy(
            send_v, rows_at(col_v, col_row(k, h), BLOCK), c_recv.at[k // FAN]
        ).start()

    for o in range(1, n_col):
        send_col((m + o) % n_col)

    @pl.when(jnp.logical_not(alone))
    def _():
        send_col(m)

    for o in range(1, FAN):
        send_row(first_group * FAN + (k + o) % FAN)

    for o in range(FAN, n_col):
        send_row(((first_group + groups - o // FAN) % groups) * FAN + (k + o) % FAN)

    def relay(g, half):
        block = rows_at(col_v, (g * 2 + half) * FAN * BLOCK, FAN * BLOCK)
        return pltpu.make_async_remote_copy(
            src_ref=block, dst_ref=block,
            send_sem=relay_send.at[g], recv_sem=relay_recv.at[g],
            device_id=(sibling, k), device_id_type=MESH,
        )

    def pass_on(g):
        block = rows_at(col_v, (g * 2 + h) * FAN * BLOCK, FAN * BLOCK)
        pltpu.make_async_copy(block, block, c_recv.at[g]).wait()
        relay(g, h).start()

    def exchange(g):
        return pltpu.make_async_remote_copy(
            src_ref=rows_at(cmsg_v, (g * 2 + 1 - h) * FAN * SLOT, FAN * SLOT),
            dst_ref=rows_at(sib_v, g * FAN * SLOT, FAN * SLOT),
            send_sem=sib_send.at[g], recv_sem=sib_recv.at[g],
            device_id=(sibling, k), device_id_type=MESH,
        )

    def row_out(c):
        return pltpu.make_async_remote_copy(
            src_ref=rows_at(rmsg_v, c * SLOT, USED), dst_ref=rows_at(rin_v, k * SLOT, USED),
            send_sem=ro_send.at[c], recv_sem=ro_recv.at[k],
            device_id=(i, c), device_id_type=MESH,
        )

    def cmsg_row(c):
        return (((c // FAN) * 2 + h) * FAN + c % FAN) * SLOT

    def col_out(c):
        return pltpu.make_async_remote_copy(
            src_ref=rows_at(cmsg_v, cmsg_row(c), USED), dst_ref=rows_at(mid_v, k * SLOT, USED),
            send_sem=co_send.at[c], recv_sem=mid_recv.at[k],
            device_id=(i, c), device_id_type=MESH,
        )

    def col_on(source):
        return pltpu.make_async_remote_copy(
            src_ref=rows_at(mid_v, source * SLOT, USED), dst_ref=rows_at(cin_v, m * SLOT, USED),
            send_sem=on_send.at[source], recv_sem=cin_recv.at[m],
            device_id=(2 * source + h, k), device_id_type=MESH,
        )

    def col_direct(c):
        return pltpu.make_async_remote_copy(
            src_ref=rows_at(cmsg_v, cmsg_row(c), USED), dst_ref=rows_at(cin_v, m * SLOT, USED),
            send_sem=co_send.at[c], recv_sem=cin_recv.at[m],
            device_id=(2 * k + h, c), device_id_type=MESH,
        )

    def send_cols(g, last):
        exchange(g).wait_recv()
        base = pl.multiple_of((g * 2 + h) * FAN * SLOT, 8)
        span = pl.ds(base, FAN * SLOT)
        cmsg_v[span] = cmsg_v[span] + sib_v[pl.ds(pl.multiple_of(g * FAN * SLOT, 8), FAN * SLOT)]

        for o in range(FAN):
            c = g * FAN + o
            stays = jnp.logical_and(alone, c == k) if last else c == k
            target, place, sems = (cin_v, m, cin_recv) if last else (mid_v, k, mid_recv)

            @pl.when(stays)
            def _():
                pltpu.make_async_copy(
                    rows_at(cmsg_v, cmsg_row(c), USED), rows_at(target, place * SLOT, USED),
                    sems.at[place],
                ).start()

            @pl.when(jnp.logical_not(stays))
            def _():
                (col_direct if last else col_out)(c).start()

    def send_on(t):
        for o in range(FAN):
            source = ((first_group + groups - t) % groups) * FAN + o
            at = rows_at(mid_v, source * SLOT, USED)
            pltpu.make_async_copy(at, at, mid_recv.at[source]).wait()

            @pl.when(source == m)
            def _():
                pltpu.make_async_copy(
                    rows_at(mid_v, m * SLOT, USED), rows_at(cin_v, m * SLOT, USED), cin_recv.at[m]
                ).start()

            @pl.when(source != m)
            def _():
                col_on(source).start()

    row_of = lax.broadcasted_iota(jnp.int32, (8, LANES), 0)
    lane_of = lax.broadcasted_iota(jnp.int32, (8, LANES), 1)
    block_of = lane_of // 16
    low_row = lax.broadcasted_iota(jnp.int32, (16, LANES), 0)
    low_lane = lax.broadcasted_iota(jnp.int32, (16, LANES), 1)
    widen = jnp.where(
        jnp.logical_and(low_lane // QUOTA == low_row % FAN, low_row < 3 * FAN), 1.0, 0.0
    ).astype(bf16)
    sum_row = lax.broadcasted_iota(jnp.int32, (8, 2 * LANES), 0)
    sum_lane = lax.broadcasted_iota(jnp.int32, (8, 2 * LANES), 1)
    gather = jnp.where((sum_lane % LANES) // QUOTA == sum_row, 1.0, 0.0).astype(bf16)

    part_v[3 * FAN * BLOCK :] = jnp.zeros((FAN * BLOCK, LANES), f32)

    pass_on(first_group)

    @pl.loop(0, groups)
    def _(t):
        g = (first_group + t) % groups

        @pl.when(t + 1 < groups)
        def _():
            pass_on((first_group + t + 1) % groups)

        relay(g, 1 - h).wait_recv()
        block = rows_at(row_v, g * FAN * BLOCK, FAN * BLOCK)
        pltpu.make_async_copy(block, block, r_recv.at[g]).wait()

        for r in range(BLOCK):
            x = col_v[pl.ds(g * (2 * FAN * BLOCK) + r, 8, stride=BLOCK), :]
            for row_bit, lane_bit in SWAPS:
                x = swap_bits(x, row_bit, lane_bit, row_of, block_of)
            right_v[8 * r : 8 * r + 8, :] = x

        value = row_v[pl.ds(pl.multiple_of(g * FAN * BLOCK, 8), FAN * BLOCK), :]
        high = value.astype(bf16).astype(f32)
        rest = value - high
        middle = rest.astype(bf16).astype(f32)
        part_v[0 : FAN * BLOCK] = high
        part_v[FAN * BLOCK : 2 * FAN * BLOCK] = middle
        part_v[2 * FAN * BLOCK : 3 * FAN * BLOCK] = rest - middle
        left_v[...] = jnp.dot(
            jnp.concatenate(
                [part_v[pl.ds(r, 16, stride=BLOCK), :].T for r in range(BLOCK)], axis=0
            ).astype(bf16),
            widen,
            preferred_element_type=f32,
        )

        @pl.when(t == 0)
        def _():
            seen_copy.wait()
            flag_copy.wait()

        sky_copy(g).wait()

        def right_of(d):
            at = (d // 8) * 8 + place_of(d % 8)
            return [
                jnp.broadcast_to(right_v[pl.ds(plane * n_dir + at, 1), :], (8, LANES))
                for plane in range(8)
            ]

        def model_step(n, total):
            for o in range(MODEL_UNROLL):
                d = n * MODEL_UNROLL + o
                right = right_of(d)
                sky = [sky_v[g, plane, d].astype(f32) for plane in range(8)]
                new = []
                for half in range(2):
                    part = [plane[8 * half : 8 * half + 8] for plane in sky]
                    left = [
                        left_v[pl.ds(pl.multiple_of((plane * n_dir + d) * n_p + 8 * half, 8), 8), :]
                        for plane in range(8)
                    ]
                    front = mul(left, part)
                    for plane in range(8):
                        front_v[plane, d, 8 * half : 8 * half + 8] = front[plane]
                        wide_sky_v[plane, d, 8 * half : 8 * half + 8] = part[plane]
                    new += mul_herm(front, right, total[8 * half : 8 * half + 8])
                total = tuple(new)
            return total

        zero = jnp.zeros((8, LANES), f32)
        model = lax.fori_loop(0, n_dir // MODEL_UNROLL, model_step, (zero,) * 16)

        @pl.when(t > 0)
        def _():
            send_cols((first_group + t + groups - 1) % groups, False)

        lanes = lanes_of(g)
        weight, error = [], []
        for half in range(2):
            rows = i * n_p + 8 * half + row_of
            columns = k * QUOTA + lane_of % QUOTA
            kept = flag_v[8 * half : 8 * half + 8, lanes].astype(f32)
            kept = kept * (rows != columns).astype(f32)
            weight.append(kept)
            for plane in range(8):
                seen = seen_v[plane, 8 * half : 8 * half + 8, lanes]
                value = kept * (seen - model[8 * half + plane])
                error.append(value)
                res_v[plane, 8 * half : 8 * half + 8, lanes] = value
        pltpu.make_async_copy(
            res_v.at[:, :, lanes], res_out.at[:, :, lanes], out_sem.at[g]
        ).start()

        def sum_step(n, carry):
            for o in range(SUM_UNROLL):
                d = n * SUM_UNROLL + o
                right = right_of(d)
                rows, cols = [], None
                for half in range(2):
                    wrong = error[8 * half : 8 * half + 8]
                    sky = [wide_sky_v[plane, d, 8 * half : 8 * half + 8] for plane in range(8)]
                    front = [front_v[plane, d, 8 * half : 8 * half + 8] for plane in range(8)]
                    behind = mul_herm(sky, right)
                    rows.append(mul_herm(wrong, behind) + [weight[half] * squares(behind)])
                    col = herm_mul(wrong, front) + [weight[half] * squares(front)]
                    cols = col if cols is None else [a + b for a, b in zip(cols, col)]
                at = pl.ds(pl.multiple_of(d * n_p, 16), n_p)
                for plane in range(9):
                    x = jnp.concatenate([rows[0][plane], rows[1][plane]], axis=0)
                    high = x.astype(bf16)
                    prod_v[plane, at, 0:LANES] = high
                    prod_v[plane, at, LANES : 2 * LANES] = (x - high.astype(f32)).astype(bf16)
                    colsum_v[plane, d] = cols[plane]
            return carry

        lax.fori_loop(0, n_dir // SUM_UNROLL, sum_step, 0)

        for plane in range(9):
            for high in range(n_dir // 8):
                items = [None] * 8
                for low in range(8):
                    items[place_of(low)] = colsum_v[plane, 8 * high + low]
                for bit in range(3):
                    up = ((row_of >> bit) & 1) == 1
                    items = [
                        jnp.where(up, b, a) + pltpu.roll(jnp.where(up, a, b), 1 << bit, 0)
                        for a, b in zip(items[0::2], items[1::2])
                    ]
                x = items[0]
                for row_bit, lane_bit in SWAPS:
                    x = swap_bits(x, row_bit, lane_bit, row_of, block_of)
                cmsg_v[pl.ds(g * 2 * FAN * SLOT + 2 * plane + high, 8, stride=SLOT), :] = x
        exchange(g).start()

        for plane in range(9):
            x = lax.dot_general(
                gather, prod_v[plane], (((1,), (1,)), ((), ())), preferred_element_type=f32
            )
            for high in range(n_dir // 8):
                rmsg_v[pl.ds(g * FAN * SLOT + 2 * plane + high, FAN, stride=SLOT), :] = x[
                    0:FAN, high * LANES : (high + 1) * LANES
                ]

        for o in range(FAN):
            c = g * FAN + o

            @pl.when(c == k)
            def _():
                pltpu.make_async_copy(
                    rows_at(rmsg_v, k * SLOT, USED), rows_at(rin_v, k * SLOT, USED), ro_recv.at[k]
                ).start()

            @pl.when(c != k)
            def _():
                row_out(c).start()

        @pl.when(t > 1)
        def _():
            send_on(t - 2)

    last_group = (first_group + groups - 1) % groups
    send_cols(last_group, True)
    for t in range(max(groups - 2, 0), groups - 1):
        send_on(t)

    def add_up(buffer, sems, source, total):
        at = rows_at(buffer, source * SLOT, USED)
        pltpu.make_async_copy(at, at, sems.at[source]).wait()
        start = pl.multiple_of(source * SLOT, 8)
        return tuple(
            part + buffer[pl.ds(start + 8 * n, size), :]
            for n, (part, size) in enumerate(zip(total, (8, 8, 2)))
        )

    def add_step(o, total):
        total = add_up(rin_v, ro_recv, (k + o) % n_col, total)
        return add_up(cin_v, cin_recv, (m + o) % n_col, total)

    zero = jnp.zeros((8, LANES), f32)
    top, bottom, curvature = lax.fori_loop(
        0, n_col, add_step, (zero, zero, jnp.zeros((2, LANES), f32))
    )
    divisor = jnp.where(
        row_of % 2 == 0,
        jnp.broadcast_to(curvature[0:1], (8, LANES)),
        jnp.broadcast_to(curvature[1:2], (8, LANES)),
    ) + epsilon
    fresh = send_v[...] + jnp.concatenate([top / divisor, bottom / divisor], axis=0)
    for j in range(8):
        wide_v[pl.ds(j, BLOCK, stride=8), :] = fresh if j == 0 else pltpu.roll(fresh, LANES - 16 * j, 1)
    new_v[...] = wide_v[:, 0:16]
    new_copy = pltpu.make_async_copy(new_v, gain_out, out_sem.at[groups])
    new_copy.start()

    sent = rows_at(row_v, 0, (n_col - 1) * BLOCK)
    pltpu.make_async_copy(sent, sent, r_send.at[0]).wait()

    @pl.when(alone)
    def _():
        sent = rows_at(row_v, 0, (n_col - 1) * BLOCK)
        pltpu.make_async_copy(sent, sent, c_send.at[0]).wait()

    @pl.when(jnp.logical_not(alone))
    def _():
        sent = rows_at(row_v, 0, n_col * BLOCK)
        pltpu.make_async_copy(sent, sent, c_send.at[0]).wait()

    @pl.loop(0, groups)
    def _(g):
        relay(g, h).wait_send()
        exchange(g).wait_send()
        lanes = lanes_of(g)
        pltpu.make_async_copy(
            res_v.at[:, :, lanes], res_out.at[:, :, lanes], out_sem.at[g]
        ).wait()

    @pl.loop(0, n_col)
    def _(c):
        @pl.when(c != k)
        def _():
            row_out(c).wait_send()

        last = c // FAN == last_group
        stays = jnp.where(last, jnp.where(alone, c, -1), c) == k

        @pl.when(jnp.logical_not(stays))
        def _():
            col_direct(c).wait_send()

        late = (c // FAN + groups - 1) % groups == first_group

        @pl.when(jnp.logical_not(jnp.logical_or(late, c == m)))
        def _():
            col_on(c).wait_send()

    new_copy.wait()


def hand_over(res_ref, gain_ref, res_out, gain_out, res_v, gain_v, sems):
    pairs = [(gain_ref, gain_v, gain_out)]
    for n in range(0, 8, 2):
        pairs.append((res_ref.at[n : n + 2], res_v.at[n : n + 2], res_out.at[n : n + 2]))
    first = [pltpu.make_async_copy(a, b, sems.at[n]) for n, (a, b, _) in enumerate(pairs)]
    second = [pltpu.make_async_copy(b, c, sems.at[5 + n]) for n, (_, b, c) in enumerate(pairs)]
    for copy in first:
        copy.start()
    for before, after in zip(first, second):
        before.wait()
        after.start()
    for copy in second:
        copy.wait()


def on_device(coherency, visibilities, flags, gains):
    n_col = lax.axis_size("col")
    n_dir, n_p, width = coherency.shape[1], coherency.shape[4], coherency.shape[5]
    groups = width // LANES
    sky = coherency.reshape(8, n_dir, n_p, width)
    seen = visibilities.reshape(8, n_p, width)
    flag = flags.reshape(n_p, width)
    mine = gains.reshape(8 * n_dir, n_p)
    f32, bf16 = jnp.float32, jnp.bfloat16
    any_spec = pl.BlockSpec(memory_space=pl.ANY)
    dma = pltpu.SemaphoreType.DMA
    residual, fresh = pl.pallas_call(
        functools.partial(kernel, n_col, n_dir, n_p),
        out_shape=(
            jax.ShapeDtypeStruct(seen.shape, f32),
            jax.ShapeDtypeStruct(mine.shape, f32),
        ),
        in_specs=[any_spec] * 4,
        out_specs=(any_spec, any_spec),
        scratch_shapes=[
            pltpu.VMEM((groups, 8, n_dir, n_p, LANES), bf16),
            pltpu.VMEM(seen.shape, f32),
            pltpu.VMEM(flag.shape, jnp.int32),
            pltpu.VMEM(mine.shape, f32),
            pltpu.VMEM((8 * n_dir, LANES), f32),
            pltpu.VMEM((BLOCK, LANES), f32),
            pltpu.VMEM((n_col * BLOCK, LANES), f32),
            pltpu.VMEM((2 * n_col * BLOCK, LANES), f32),
            pltpu.VMEM((4 * FAN * BLOCK, LANES), f32),
            pltpu.VMEM((8 * n_dir * n_p, LANES), f32),
            pltpu.VMEM((8 * n_dir, LANES), f32),
            pltpu.VMEM((8, n_dir, n_p, LANES), f32),
            pltpu.VMEM((8, n_dir, n_p, LANES), f32),
            pltpu.VMEM(seen.shape, f32),
            pltpu.VMEM((9, n_dir * n_p, 2 * LANES), bf16),
            pltpu.VMEM((9, n_dir, 8, LANES), f32),
            pltpu.VMEM((n_col * SLOT, LANES), f32),
            pltpu.VMEM((2 * n_col * SLOT, LANES), f32),
            pltpu.VMEM((n_col * SLOT, LANES), f32),
            pltpu.VMEM((n_col * SLOT, LANES), f32),
            pltpu.VMEM((n_col * SLOT, LANES), f32),
            pltpu.VMEM((n_col * SLOT, LANES), f32),
            pltpu.VMEM(mine.shape, f32),
            dma((3 + groups,)),
            dma((1,)),
            dma((1,)),
            dma((groups,)),
            dma((groups,)),
            dma((groups,)),
            dma((groups,)),
            dma((groups,)),
            dma((groups,)),
            dma((n_col,)),
            dma((n_col,)),
            dma((n_col,)),
            dma((n_col,)),
            dma((n_col,)),
            dma((n_col,)),
            dma((groups + 1,)),
        ],
        compiler_params=pltpu.CompilerParams(
            collective_id=0, has_side_effects=True, vmem_limit_bytes=56 * 1024 * 1024
        ),
    )(sky, seen, flag, mine)
    residual, fresh = pl.pallas_call(
        hand_over,
        out_shape=(
            jax.ShapeDtypeStruct(seen.shape, f32),
            jax.ShapeDtypeStruct(mine.shape, f32),
        ),
        in_specs=[any_spec] * 2,
        out_specs=(any_spec, any_spec),
        scratch_shapes=[pltpu.VMEM(seen.shape, f32), pltpu.VMEM(mine.shape, f32), dma((10,))],
        compiler_params=pltpu.CompilerParams(vmem_limit_bytes=56 * 1024 * 1024),
    )(residual, fresh)
    return residual.reshape(visibilities.shape), fresh.reshape(gains.shape)


def solution(mesh):
    return jax.shard_map(
        on_device,
        mesh=mesh,
        in_specs=(
            P(None, None, None, "col", "row", None),
            P(None, None, "col", "row", None),
            P(None, "col", "row", None),
            P(None, None, "col", "row"),
        ),
        out_specs=(P(None, None, "col", "row", None), P(None, None, "col", "row")),
        check_vma=False,
    )
```
